256 devices in a mesh: mode: 8 (over z_hi, y), space: 32 (over x, z_lo, core).
Axes of the slice: x: 4, y: 4, z: 8 (z_hi: 2, z_lo: 4; z = z_hi * 4 + z_lo), core: 2. Of those that a mesh axis runs over, the one named last changes fastest.
Arguments:
- energy: float32 [128, 256, 16, 128], P('mode', 'space'), may hold values from -6 to 6
- void: int32 [256, 16, 128], P('space'), may hold values 0 or 1
- spacing_cells: float32 [256, 16, 128], P('space'), may hold values from 2 to 50
- walls: int32 [2, 256, 128], P(None, 'space'), may hold values from 0 to 2
- octant: int32 [128], replicated, may hold values from 0 to 7
- specific_warmth_modes: float32 [128], replicated, may hold values from 0.2 to 2
- second_derivative: float32 [128], replicated, may hold values from 0.5 to 1.5
- umklapp: float32 [128], replicated, may hold values from 0.02 to 1
- isotope: float32 [128], replicated, may hold values from 0.01 to 0.3
- courant: float32 [3, 128], replicated, may hold values from 0.05 to 0.9
Outputs:
- final_energy: float32 [128, 256, 16, 128], P('mode', 'space')
- prior_pseudo_kelvin: float32 [256, 16, 128], P('space')
The draws below stay inside these ranges and needn't reach their ends.
Inputs may be any that keep to these rules, and one draw needn't show every extreme that they name: `walls`: 0 adiabatic wall, 1 cold black wall, 2 hot black wall. `octant`: bit 0, 1 and 2 give a negative direction along the first, second and third dimension.
All inputs are finite; a program needn't handle non-finite values. No bound on the sum of `void` on one device may be relied on, other than what follows from the above.
Results may differ from the reference program's by a relative error of at most 0.0003.
Values sent between devices are 32-bit elements; how exact they have to be, the bound alone decides.
A program may use at most 64 MiB of HBM per device.

```python
import math
import jax
import jax.numpy as jnp
from jax import lax

MODES = 128
NZ = 16
NY = 128
ITERS = 8
STEPS = 1
NX = 256


def with_ends(values, key, least, high):
    shape = values.shape
    place = [jax.random.randint(jax.random.fold_in(key, axis), (), 0, shape[axis]) for axis in range(len(shape))]
    values = values.at[tuple(place)].set(least)
    longest = shape.index(max(shape))
    place[longest] = (place[longest] + 1) % shape[longest]
    return values.at[tuple(place)].set(high)


def block_scale(stream_key, extent, cuts, smallest, top_value):
    factor_of = 1.0
    for axis_at, blocks in cuts:
        heights = jax.random.uniform(jax.random.fold_in(jax.random.fold_in(stream_key, 6), axis_at), (blocks,), jnp.float32, smallest / len(cuts), top_value / len(cuts))
        factor_of = factor_of * jnp.repeat(jnp.exp(heights), extent[axis_at] // blocks).reshape((-1,) + (1,) * (len(extent) - 1 - axis_at))
    return factor_of


def noise(rng, shape, deviation, limit, pieces=(), dtype=jnp.bfloat16):
    gain = block_scale(rng, shape, pieces, -0.22, 0.18) if pieces else 1.0
    drawn = jax.random.normal(rng, shape, jnp.float32) * deviation * gain
    return jnp.minimum(jnp.maximum(drawn, -limit), limit).astype(dtype)


def setup_inputs(seed: int = 0) -> dict:
    key_list = jax.random.split(jax.random.key(seed), 11)
    energy = noise(key_list[0], (MODES, NX, NZ, NY), 1.0, 6.0, ((0, 8), (1, 32)), jnp.float32)
    void = with_ends((jax.random.randint(key_list[1], (NX, NZ, NY), 0, 8) < 1).astype(jnp.int32), jax.random.fold_in(key_list[1], 1), 0, 1)
    spacing_cells = jnp.clip(jnp.exp(math.log(50.0) - 3.218876 * jax.random.uniform(key_list[2], (NX, NZ, NY), jnp.float32) ** block_scale(key_list[2], (NX, NZ, NY), ((0, 32),), -0.2, 0.2)), 2.0, 50.0)
    walls = with_ends(jax.random.randint(key_list[3], (2, NX, NY), 0, 3), jax.random.fold_in(key_list[3], 1), 0, 2).astype(jnp.int32)
    octant = with_ends(jax.random.randint(key_list[4], (MODES,), 0, 8), jax.random.fold_in(key_list[4], 1), 0, 7).astype(jnp.int32)
    specific_warmth_modes = jnp.clip(jnp.exp(jax.random.uniform(key_list[5], (MODES,), jnp.float32, math.log(0.2), math.log(2.0))), 0.2, 2.0)
    second_derivative = jnp.clip(jax.random.uniform(key_list[6], (MODES,), jnp.float32, 0.5, 1.5), 0.5, 1.5)
    umklapp = jnp.clip(jnp.exp(jax.random.uniform(key_list[7], (MODES,), jnp.float32, math.log(0.02), math.log(1.0))), 0.02, 1.0)
    isotope = jnp.clip(jnp.exp(jax.random.uniform(key_list[8], (MODES,), jnp.float32, math.log(0.01), math.log(0.3))), 0.01, 0.3)
    courant = jnp.clip(jnp.exp(jax.random.uniform(key_list[9], (3, MODES), jnp.float32, math.log(0.05), math.log(0.9))), 0.05, 0.9)
    return {"energy": energy, "void": void, "spacing_cells": spacing_cells, "walls": walls, "octant": octant, "specific_warmth_modes": specific_warmth_modes, "second_derivative": second_derivative, "umklapp": umklapp, "isotope": isotope, "courant": courant}


RELAX_WEIGHT = 0.35
HOT_WALL = 1.0

def broadcast_modes(vector):
    return vector[:, None, None, None]

def mode_signs(octant):
    sign_x = 1 - 2 * (octant % 2)
    sign_y = 1 - 2 * (octant // 2 % 2)
    sign_z = 1 - 2 * (octant // 4)
    return (sign_x, sign_y, sign_z)

def transfer_rate(umklapp, isotope, speed, spacing_cells):
    rate = broadcast_modes(umklapp + isotope) + broadcast_modes(speed) / spacing_cells[None]
    return 1.0 - jnp.exp(-rate)

def rest_population(specific_warmth_modes, second_derivative, prior_pseudo_kelvin):
    weighted_quantity = broadcast_modes(second_derivative) * prior_pseudo_kelvin[None]
    return (broadcast_modes(specific_warmth_modes / second_derivative) * jnp.sinh(weighted_quantity), broadcast_modes(specific_warmth_modes) * jnp.cosh(weighted_quantity))

def beam_update(field, near, far, courant_band):
    factor = broadcast_modes(courant_band)
    return field - 0.5 * factor * (3.0 * field - 4.0 * near + far) + 0.5 * factor * factor * (field - 2.0 * near + far)

def beam_rolled(field, courant_band, sign, axis):
    forward = broadcast_modes(sign) > 0
    near = jnp.where(forward, jnp.roll(field, 1, axis), jnp.roll(field, -1, axis))
    far = jnp.where(forward, jnp.roll(field, 2, axis), jnp.roll(field, -2, axis))
    return beam_update(field, near, far, courant_band)

def wall_sweep(field, courant_band, sign, walls, specific_warmth_modes, second_derivative):
    factor = broadcast_modes(courant_band)
    forward = broadcast_modes(sign) > 0
    inflow = broadcast_modes(specific_warmth_modes / second_derivative * jnp.sinh(second_derivative * HOT_WALL))
    bottom = jnp.where(walls[0] == 2, 1.0, 0.0)[None, :, None, :] * inflow
    upper = jnp.where(walls[1] == 2, 1.0, 0.0)[None, :, None, :] * inflow
    from_below = jnp.concatenate([bottom, field[:, :, :-1]], axis=2)
    from_above = jnp.concatenate([field[:, :, 1:], upper], axis=2)
    upstream = jnp.where(forward, from_below, from_above)
    depth = lax.broadcasted_iota(jnp.int32, (1, 1, field.shape[2], 1), 2)
    block_top = (depth == field.shape[2] - 1) & (walls[1] == 0)[None, :, None, :]
    block_bottom = (depth == 0) & (walls[0] == 0)[None, :, None, :]
    blocked = jnp.where(forward, block_top, block_bottom)
    outflow = jnp.where(blocked, 0.0, factor * field)
    return field - outflow + factor * upstream

def reference(energy, void, spacing_cells, walls, octant, specific_warmth_modes, second_derivative, umklapp, isotope, courant):
    fluid = (1 - void).astype(jnp.float32)
    sign_x, sign_y, sign_z = mode_signs(octant)
    speed = jnp.sqrt(lax.optimization_barrier(jnp.sum(courant * courant, axis=0)))
    relax = transfer_rate(umklapp, isotope, speed, spacing_cells)
    iterate_carry = energy * fluid[None]
    prior_pseudo_kelvin = jnp.zeros(spacing_cells.shape, jnp.float32)
    for step in range(STEPS):
        prior_pseudo_kelvin = jnp.zeros(spacing_cells.shape, jnp.float32)
        for sweep in range(ITERS):
            matrix_element, derivative_of_content = rest_population(specific_warmth_modes, second_derivative, prior_pseudo_kelvin)
            balance_mismatch = lax.optimization_barrier(jnp.sum(relax * (matrix_element - iterate_carry), axis=0))
            combined_derivative = lax.optimization_barrier(jnp.sum(relax * derivative_of_content, axis=0))
            prior_pseudo_kelvin = prior_pseudo_kelvin - RELAX_WEIGHT * balance_mismatch / combined_derivative
        matrix_element, derivative_of_content = rest_population(specific_warmth_modes, second_derivative, prior_pseudo_kelvin)
        iterate_carry = iterate_carry + relax * (matrix_element - iterate_carry)
        iterate_carry = beam_rolled(iterate_carry, courant[0], sign_x, 1)
        iterate_carry = wall_sweep(iterate_carry, courant[2], sign_z, walls, specific_warmth_modes, second_derivative)
        iterate_carry = beam_rolled(iterate_carry, courant[1], sign_y, 3)
        iterate_carry = iterate_carry * fluid[None]
    return (iterate_carry, prior_pseudo_kelvin)
```

```python
import functools
import math

import jax
import jax.numpy as jnp
from jax import lax
from jax.experimental import pallas as pl
from jax.experimental.pallas import tpu as pltpu
from jax.sharding import PartitionSpec as P

MESH = pl.DeviceIdType.MESH
ITERS = 8
RELAX_WEIGHT = 0.35
HOT_WALL = 1.0
TERMS = 22
RATE_TERMS = 12
SCALE = 8.0
F32 = jnp.float32

(N_RATE, N_SPEED, WARM_HALF, CURVE, GO_X, GO_Y, GO_Z, X0, X1, X2, CZ, Y0, Y1, Y2, HOT) = range(15)


def sweep_factors(c):
    return 1.0 - 1.5 * c + 0.5 * c * c, 2.0 * c - c * c, 0.5 * c * c - 0.5 * c


def kernel(
    space,
    energy, void, spacing, walls, octant, warmth, curve, umklapp, isotope, courant,
    out, temp_out,
    st, sp, vd, wl, oc, pv, cr, fl, up_keep, dn_keep, bot, top,
    part, got, mu, zt, tab, uu, ww, tp, res,
    in_sem, small_sem, rs_send, rs_recv, t_send, t_recv, h_send, h_recv, out_sem, l_sem, g_sem, go_sem,
):
    m, s = lax.axis_index("mode"), lax.axis_index("space")
    left, right = lax.rem(s + space - 1, space), lax.rem(s + 1, space)
    y = lax.rem(m, 4)
    early = m < 4
    late = m >= 4

    def signal(sem, mode, strip):
        pl.semaphore_signal(sem, inc=1, device_id=(mode, strip), device_id_type=MESH)

    small = [
        pltpu.make_async_copy(src, dst, small_sem.at[i])
        for i, (src, dst) in enumerate(
            (
                (spacing, sp.at[pl.ds(2, 8)]),
                (void, vd),
                (umklapp, pv.at[pl.ds(0, 1)]),
                (isotope, pv.at[pl.ds(8, 1)]),
                (courant, cr),
                (warmth, pv.at[pl.ds(16, 1)]),
                (curve, pv.at[pl.ds(24, 1)]),
                (octant, oc),
                (walls, wl),
            )
        )
    ]
    loads = [
        pltpu.make_async_copy(
            energy.at[:, pl.ds(4 * i, 4)], st.at[:, pl.ds(2 + 4 * i, 4)], in_sem.at[i]
        )
        for i in range(2)
    ]
    for c in small[:5]:
        c.start()
    for c in loads:
        c.start()
    for c in small[5:]:
        c.start()

    barrier = pltpu.get_barrier_semaphore()

    @pl.when(early)
    def _():
        for j in range(1, 8):
            signal(barrier, lax.rem(m + j, 8), s)
        for strip in (left, right):
            signal(barrier, y, strip)
            signal(barrier, 4 + y, strip)

    @pl.when(m == 0)
    def _():
        for k in range(8):
            signal(barrier, k, left)

    @pl.when(m == 2)
    def _():
        for k in range(8):
            signal(barrier, k, right)

    for c in small[:5]:
        c.wait()

    lane = lax.broadcasted_iota(jnp.int32, (16, 128), 1)
    band = lax.broadcasted_iota(jnp.int32, (16, 128), 0) + 16 * m

    def own(vector):
        picked = jnp.where(lane == band, jnp.broadcast_to(vector, (16, 128)), 0.0)
        return jnp.broadcast_to(jnp.sum(picked, axis=1, keepdims=True), (16, 128))

    rate = pv[0:1, :] + pv[8:9, :]
    cx, cy, cz = cr[0:1, :], cr[1:2, :], cr[2:3, :]
    speed = jnp.sqrt(cx * cx + cy * cy + cz * cz)
    tab[N_RATE] = own(-rate)
    tab[N_SPEED] = own(-speed)

    pl.semaphore_wait(barrier, jnp.where(early, 7, 8))

    @pl.when(late)
    def _():
        for strip in (s, left, right):
            signal(g_sem, y, strip)
        for k in range(4):
            signal(l_sem, k, s)

    def row(table, b):
        return tab[table, pl.ds(b, 1), :]

    def pass_one(r, carry):
        inverse = 1.0 / sp[2 + r]
        total = jnp.zeros((16, 128), F32)
        for b in range(16):
            kept = jnp.exp(row(N_RATE, b) + row(N_SPEED, b) * inverse)
            total = total + (1.0 - kept) * st[b, 2 + r]
        fluid = (1 - vd[r]).astype(F32)
        fl[r] = fluid
        part[r] = total * fluid
        return carry

    sends = []

    def send(first, count, mode, strip, i, when):
        c = pltpu.make_async_remote_copy(
            part.at[pl.ds(first, count)],
            got.at[m, pl.ds(0, count)],
            rs_send.at[i],
            rs_recv.at[m],
            device_id=(mode, strip),
            device_id_type=MESH,
        )
        sends.append((c, when))
        if when is None:
            c.start()
        else:
            pl.when(when)(c.start)

    loads[0].wait()
    lax.fori_loop(0, 4, pass_one, 0)
    send(0, 4, 1, s, 0, m != 1)
    send(0, 2, 2, left, 1, None)
    loads[1].wait()
    lax.fori_loop(4, 8, pass_one, 0)
    send(4, 4, 3, s, 2, m != 3)
    send(6, 2, 0, right, 3, None)

    @pl.when(m == 1)
    def _():
        got[1] = part[0:4]

    @pl.when(m == 3)
    def _():
        got[3] = part[4:8]

    for c in small[5:]:
        c.wait()

    warm, bend = pv[16:17, :], pv[24:25, :]
    own_warm, own_bend = own(warm), own(bend)
    tab[WARM_HALF] = 0.5 * own_warm / own_bend
    tab[CURVE] = own_bend
    tab[HOT] = (0.5 * own_warm / own_bend) * (jnp.exp(own_bend * HOT_WALL) - jnp.exp(-own_bend * HOT_WALL))
    octants = own(oc[0:1, :].astype(F32)).astype(jnp.int32)
    tab[GO_X] = (1 - lax.rem(octants, 2)).astype(F32)
    tab[GO_Y] = (1 - lax.rem(octants // 2, 2)).astype(F32)
    tab[GO_Z] = (1 - octants // 4).astype(F32)
    tab[X0], tab[X1], tab[X2] = sweep_factors(own(cx))
    tab[Y0], tab[Y1], tab[Y2] = sweep_factors(own(cy))
    tab[CZ] = own(cz)

    def weights(p, b, held, inverse):
        kept = jnp.exp(row(N_RATE, b) + row(N_SPEED, b) * inverse)
        uu[b, p] = kept * held
        ww[b, p] = (1.0 - kept) * row(WARM_HALF, b)

    def pass_two(r, carry):
        inverse = 1.0 / sp[2 + r]
        fluid = fl[r]
        for b in range(16):
            held = st[b, 2 + r] * fluid
            st[b, 2 + r] = held
            weights(2 + r, b, held, inverse)
        return carry

    lax.fori_loop(0, 8, pass_two, 0)

    halos = []
    for i, (src, dst, strip) in enumerate(((8, 0, right), (2, 10, left))):
        for j, (a, b) in enumerate(
            (
                (sp.at[pl.ds(src, 2)], sp.at[pl.ds(dst, 2)]),
                (st.at[:, pl.ds(src, 2)], st.at[:, pl.ds(dst, 2)]),
            )
        ):
            halos.append(
                pltpu.make_async_remote_copy(
                    a, b, h_send.at[2 * i + j], h_recv.at[2 * i + j], device_id=(m, strip), device_id_type=MESH
                )
            )

    @pl.when(early)
    def _():
        for c in halos:
            c.start()

    depth = lax.broadcasted_iota(jnp.int32, (16, 128), 0)

    def wall_rows(r, carry):
        low = jnp.broadcast_to(wl[0, pl.ds(r, 1), :], (16, 128))
        high = jnp.broadcast_to(wl[1, pl.ds(r, 1), :], (16, 128))
        up_keep[r] = jnp.where((depth == 15) & (high == 0), 0.0, 1.0)
        dn_keep[r] = jnp.where((depth == 0) & (low == 0), 0.0, 1.0)
        bot[r] = jnp.where((depth == 0) & (low == 2), 1.0, 0.0)
        top[r] = jnp.where((depth == 15) & (high == 2), 1.0, 0.0)
        return carry

    lax.fori_loop(0, 8, wall_rows, 0)

    def series():
        order = lax.broadcasted_iota(jnp.int32, (16, 128), 0)
        rest = jnp.exp(-rate)
        powers = jnp.zeros((16, 128), F32)
        term = -rest
        for j in range(RATE_TERMS):
            value = 1.0 - rest if j == 0 else term
            powers = jnp.where(order == j, jnp.broadcast_to(value, (16, 128)), powers)
            term = term * (-speed) * (1.0 / (j + 1))
        weight = warm
        for k in range(TERMS):
            summed = jnp.sum(powers * weight, axis=1, keepdims=True)
            zt[k] = jnp.broadcast_to(summed, (16, 128))
            weight = weight * (bend * bend) * (SCALE * SCALE / ((2 * k + 2) * (2 * k + 3)))

    def moments(p, i):
        inverse = 1.0 / sp[p]
        for k in range(TERMS):
            value = jnp.broadcast_to(zt[k, RATE_TERMS - 1 : RATE_TERMS, :], (16, 128))
            for j in range(RATE_TERMS - 2, -1, -1):
                value = value * inverse + zt[k, j : j + 1, :]
            mu[k, i] = value

    def own_rows(base, count, peers):
        def one(i, carry):
            moments(base + i, i)
            return carry

        lax.fori_loop(0, count, one, 0)
        pl.semaphore_wait(g_sem, 3)
        signal(go_sem, 4 + y, s)
        for k in peers:
            pltpu.make_async_remote_copy(
                part.at[pl.ds(0, count)], got.at[k, pl.ds(0, count)], rs_send.at[0], rs_recv.at[k],
                device_id=(m, s), device_id_type=MESH,
            ).wait_recv()
        total = got[0, 0:count]
        for k in range(1, 8):
            total = total + got[k, 0:count]
        t = RELAX_WEIGHT * total / mu[0, 0:count]

        def iterate(_, t):
            q = (t * (1.0 / SCALE)) * (t * (1.0 / SCALE))
            value = mu[TERMS - 1, 0:count]
            slope = value
            for k in range(TERMS - 2, -1, -1):
                value = value * q + mu[k, 0:count]
                if k > 0:
                    slope = slope * q + value
            return t - RELAX_WEIGHT * (t * value - total) / (value + 2.0 * q * slope)

        t = lax.fori_loop(1, ITERS, iterate, t)
        tp[base : base + count] = t

    OWNED = {0: (0, 2), 1: (2, 4), 3: (6, 4), 2: (10, 2)}

    def t_copy(owner, mode, i):
        base, count = OWNED[owner]
        return pltpu.make_async_remote_copy(
            tp.at[pl.ds(base, count)], tp.at[pl.ds(base, count)], t_send.at[i], t_recv.at[owner],
            device_id=(mode, s), device_id_type=MESH,
        )

    pl.when(early)(series)
    for owner in range(4):
        @pl.when(m == owner)
        def _(owner=owner):
            base, count = OWNED[owner]
            if owner == 0:
                halos[0].wait_recv()
            if owner == 2:
                halos[2].wait_recv()
            own_rows(base, count, [k for k in range(8) if count == 2 or k != owner])
            for j in range(1, 4):
                t_copy(owner, (owner + j) % 4, j).start()
            pl.semaphore_wait(l_sem, 4)
            for j in range(4):
                t_copy(owner, 4 + j, 4 + j).start()

    @pl.when(late)
    def _():
        pl.semaphore_wait(go_sem, 1)
        for c in halos:
            c.start()

    def halo_rows(first):
        for p in (first, first + 1):
            inverse = 1.0 / sp[p]
            for b in range(16):
                weights(p, b, st[b, p], inverse)

    for i, c in enumerate(halos):
        if i == 0:
            pl.when(m != 0)(c.wait_recv)
        elif i == 2:
            pl.when(m != 2)(c.wait_recv)
        else:
            c.wait_recv()
            halo_rows((0, 10)[i // 2])

    for owner in range(4):
        pl.when(m != owner)(t_copy(owner, owner, 0).wait_recv)

    def relaxed(p, b, bend):
        x = tp[p] * bend
        return uu[b, p] + ww[b, p] * (jnp.exp(x) - jnp.exp(-x))

    def sweep(b, carry):
        bend = row(CURVE, b)
        go_x = jnp.broadcast_to(row(GO_X, b), (16, 128)) > 0.5
        go_y = jnp.broadcast_to(row(GO_Y, b), (16, 128)) > 0.5
        go_z = jnp.broadcast_to(row(GO_Z, b), (16, 128)) > 0.5
        inflow = jnp.where(go_z, depth, 15 - depth) == 0
        cells = {p: relaxed(p, b, bend) for p in range(2, 10)}
        for p, q in ((1, 10), (0, 11)):
            x = jnp.where(go_x, tp[p], tp[q]) * bend
            cells[p] = cells[q] = jnp.where(go_x, uu[b, p], uu[b, q]) + jnp.where(go_x, ww[b, p], ww[b, q]) * (
                jnp.exp(x) - jnp.exp(-x)
            )
        for r in range(8):
            p = r + 2
            near = jnp.where(go_x, cells[p - 1], cells[p + 1])
            far = jnp.where(go_x, cells[p - 2], cells[p + 2])
            a = row(X0, b) * cells[p] + row(X1, b) * near + row(X2, b) * far
            up = jnp.where(go_z, pltpu.roll(a, 1, 0), pltpu.roll(a, 15, 0))
            hot = jnp.where(go_z, bot[r], top[r]) * row(HOT, b)
            up = jnp.where(inflow, hot, up)
            keep = jnp.where(go_z, up_keep[r], dn_keep[r])
            a = a + row(CZ, b) * (up - keep * a)
            near = jnp.where(go_y, pltpu.roll(a, 1, 1), pltpu.roll(a, 127, 1))
            far = jnp.where(go_y, pltpu.roll(a, 2, 1), pltpu.roll(a, 126, 1))
            res[b, r] = (row(Y0, b) * a + row(Y1, b) * near + row(Y2, b) * far) * fl[r]
        pltpu.make_async_copy(res.at[b], out.at[b], out_sem.at[b]).start()
        return carry

    lax.fori_loop(0, 16, sweep, 0)
    last = pltpu.make_async_copy(tp.at[pl.ds(2, 8)], temp_out, out_sem.at[16])
    last.start()
    for b in range(16):
        pltpu.make_async_copy(res.at[b], out.at[b], out_sem.at[b]).wait()
    last.wait()
    for c, when in sends:
        if when is None:
            c.wait_send()
        else:
            pl.when(when)(c.wait_send)
    for c in halos:
        c.wait_send()
    for owner in range(4):
        @pl.when(m == owner)
        def _(owner=owner):
            for j in range(1, 8):
                t_copy(owner, owner, j).wait_send()


def solution(mesh):
    space = mesh.shape["space"]

    def local(energy, void, spacing, walls, octant, warmth, curve, umklapp, isotope, courant):
        flat = lambda v: v.reshape(1, 128)
        any_space = pl.BlockSpec(memory_space=pl.ANY)
        dma = pltpu.SemaphoreType.DMA
        regular = pltpu.SemaphoreType.REGULAR
        return pl.pallas_call(
            functools.partial(kernel, space),
            out_shape=(
                jax.ShapeDtypeStruct(energy.shape, F32),
                jax.ShapeDtypeStruct(spacing.shape, F32),
            ),
            in_specs=[pl.BlockSpec(memory_space=pltpu.HBM)] * 10,
            out_specs=(any_space, any_space),
            scratch_shapes=[
                pltpu.VMEM((16, 12, 16, 128), F32),
                pltpu.VMEM((12, 16, 128), F32),
                pltpu.VMEM((8, 16, 128), jnp.int32),
                pltpu.VMEM((2, 8, 128), jnp.int32),
                pltpu.VMEM((1, 128), jnp.int32),
                pltpu.VMEM((32, 128), F32),
                pltpu.VMEM((3, 128), F32),
            ]
            + [pltpu.VMEM((8, 16, 128), F32)] * 5
            + [
                pltpu.VMEM((8, 16, 128), F32),
                pltpu.VMEM((8, 4, 16, 128), F32),
                pltpu.VMEM((TERMS, 4, 16, 128), F32),
                pltpu.VMEM((TERMS, 16, 128), F32),
                pltpu.VMEM((15, 16, 128), F32),
                pltpu.VMEM((16, 12, 16, 128), F32),
                pltpu.VMEM((16, 12, 16, 128), F32),
                pltpu.VMEM((12, 16, 128), F32),
                pltpu.VMEM((16, 8, 16, 128), F32),
                dma((2,)),
                dma((9,)),
                dma((4,)),
                dma((8,)),
                dma((8,)),
                dma((4,)),
                dma((4,)),
                dma((4,)),
                dma((17,)),
                regular,
                regular,
                regular,
            ],
            compiler_params=pltpu.CompilerParams(
                collective_id=0, has_side_effects=True, vmem_limit_bytes=32 * 1024 * 1024
            ),
        )(
            *[
                pltpu.with_memory_space_constraint(v, pltpu.HBM)
                for v in (
                    energy, void, spacing, walls, flat(octant), flat(warmth), flat(curve), flat(umklapp),
                    flat(isotope), courant,
                )
            ]
        )

    in_specs = (
        P("mode", "space", None, None),
        P("space", None, None),
        P("space", None, None),
        P(None, "space", None),
        P(),
        P(),
        P(),
        P(),
        P(),
        P(),
    )
    out_specs = (P("mode", "space", None, None), P("space", None, None))
    return jax.shard_map(local, mesh=mesh, in_specs=in_specs, out_specs=out_specs, check_vma=False)
```

```python
import functools
import math

import jax
import jax.numpy as jnp
from jax import lax
from jax.experimental import pallas as pl
from jax.experimental.pallas import tpu as pltpu
from jax.sharding import PartitionSpec as P

MESH = pl.DeviceIdType.MESH
ITERS = 8
RELAX_WEIGHT = 0.35
HOT_WALL = 1.0
RUN = 8
TERMS = 22
RATE_TERMS = 12
SCALE = 8.0
F32 = jnp.float32

(N_RATE, N_SPEED, WARM_HALF, CURVE, GO_X, GO_Z, X0, X1, X2, CZ, Y0, Y1, Y2, HOT) = range(14)


def sweep_factors(c):
    return 1.0 - 1.5 * c + 0.5 * c * c, 2.0 * c - c * c, 0.5 * c * c - 0.5 * c


PIECES = ((0, 2, 2, 1, True), (1, 3, 0, 3, True), (2, 6, 0, 3, True), (3, 9, 0, 1, True), (0, 0, 0, 2, False), (3, 10, 1, 2, False))
INNER, OUTER = (2, 3, 4, 5), (0, 1, 6, 7)


def relaxed(t, held, pull, bend):
    x = t * bend
    return held + pull * (jnp.exp2(x) - jnp.exp2(-x))


def across(b, row, cells, rows, walls, state):
    up_keep, dn_keep, bot, top = walls
    depth = lax.broadcasted_iota(jnp.int32, (16, 128), 0)
    go_x = jnp.broadcast_to(row(GO_X, b), (16, 128)) > 0.5
    go_z = jnp.broadcast_to(row(GO_Z, b), (16, 128)) > 0.5
    inflow = jnp.where(go_z, depth, 15 - depth) == 0
    for i, r in enumerate(rows):
        p = r + 2
        near = jnp.where(go_x, cells[p - 1], cells[p + 1])
        far = jnp.where(go_x, cells[p - 2], cells[p + 2])
        a = row(X0, b) * cells[p] + row(X1, b) * near + row(X2, b) * far
        up = jnp.where(go_z, pltpu.roll(a, 1, 0), pltpu.roll(a, 15, 0))
        up = jnp.where(inflow, jnp.where(go_z, bot[r], top[r]) * row(HOT, b), up)
        keep = jnp.where(go_z, up_keep[r], dn_keep[r])
        state[b, i] = a + row(CZ, b) * (up - keep * a)


def along(b, row, octant, rows, fl, state, res):
    shift = jnp.where((octant & 2) == 0, 1, 127)
    twice = jnp.where((octant & 2) == 0, 2, 126)
    for i, r in enumerate(rows):
        a = state[b, i]
        near, far = pltpu.roll(a, shift, 1), pltpu.roll(a, twice, 1)
        res[b, i] = (row(Y0, b) * a + row(Y1, b) * near + row(Y2, b) * far) * fl[r]


def kernel(
    space,
    energy, void, spacing, walls, octant, warmth, curve, umklapp, isotope, courant,
    uu, ww, tp, fl, up_keep, dn_keep, bot, top, tab, oc, res,
    state, octants, st, sp, vd, wl, pv, cr, part, got, mu, zt,
    in_sem, small_sem, rs_send, rs_recv, own_recv, t_send, t_recv, h_send, h_recv, l_sem, left_sem, right_sem,
):
    m, s = lax.axis_index("mode"), lax.axis_index("space")
    left, right = lax.rem(s + space - 1, space), lax.rem(s + 1, space)
    y = lax.rem(m, 4)
    early = m < 4
    late = m >= 4

    def signal(sem, mode, strip):
        pl.semaphore_signal(sem, inc=1, device_id=(mode, strip), device_id_type=MESH)

    small = [
        pltpu.make_async_copy(src, dst, small_sem.at[i])
        for i, (src, dst) in enumerate(
            (
                (spacing, sp.at[pl.ds(2, 8)]),
                (void, vd),
                (umklapp, pv.at[pl.ds(0, 1)]),
                (isotope, pv.at[pl.ds(8, 1)]),
                (courant, cr),
                (warmth, pv.at[pl.ds(16, 1)]),
                (curve, pv.at[pl.ds(24, 1)]),
                (octant, oc),
                (walls, wl),
                (octant, octants),
            )
        )
    ]
    loads = [
        pltpu.make_async_copy(
            energy.at[:, pl.ds(4 * i, 4)], st.at[:, pl.ds(2 + 4 * i, 4)], in_sem.at[i]
        )
        for i in range(2)
    ]
    for c in small[:5]:
        c.start()
    for c in loads:
        c.start()
    for c in small[5:]:
        c.start()

    barrier = pltpu.get_barrier_semaphore()

    @pl.when(early)
    def _():
        for j in range(1, 8):
            signal(barrier, lax.rem(m + j, 8), s)
        for strip in (left, right):
            signal(barrier, y, strip)

    @pl.when(m == 0)
    def _():
        for k in range(8):
            signal(barrier, k, left)

    @pl.when(m == 3)
    def _():
        for k in range(8):
            signal(barrier, k, right)

    place = lax.rem(s, RUN)
    leads, trails = place == 0, place == RUN - 1

    @pl.when(late & ~trails)
    def _():
        signal(barrier, m, right)

    @pl.when(late & leads)
    def _():
        signal(barrier, m, left)

    for c in small[:5]:
        c.wait()

    lane = lax.broadcasted_iota(jnp.int32, (16, 128), 1)
    band = lax.broadcasted_iota(jnp.int32, (16, 128), 0) + 16 * m

    def own(vector):
        picked = jnp.where(lane == band, jnp.broadcast_to(vector, (16, 128)), 0.0)
        return jnp.broadcast_to(jnp.sum(picked, axis=1, keepdims=True), (16, 128))

    rate = pv[0:1, :] + pv[8:9, :]
    cx, cy, cz = cr[0:1, :], cr[1:2, :], cr[2:3, :]
    speed = jnp.sqrt(cx * cx + cy * cy + cz * cz)
    tab[N_RATE] = own(-rate)
    tab[N_SPEED] = own(-speed)

    pl.semaphore_wait(barrier, jnp.where(early, 7, 7 + trails.astype(jnp.int32) - leads.astype(jnp.int32)))

    @pl.when(late)
    def _():
        for k in range(4):
            signal(l_sem, k, s)

    @pl.when(late & ~leads)
    def _():
        signal(right_sem, m, left)

    @pl.when(late & trails)
    def _():
        signal(left_sem, m, right)

    def row(table, b):
        return tab[table, pl.ds(b, 1), :]

    def pass_one(r, carry):
        inverse = 1.0 / sp[2 + r]
        total = jnp.zeros((16, 128), F32)
        for b in range(16):
            kept = jnp.exp(row(N_RATE, b) + row(N_SPEED, b) * inverse)
            total = total + (1.0 - kept) * st[b, 2 + r]
        fluid = (1 - vd[r]).astype(F32)
        fl[r] = fluid
        part[r] = total * fluid
        return carry

    sends = []

    def send(first, count, slot, mode, strip, i, recv, when):
        c = pltpu.make_async_remote_copy(
            part.at[pl.ds(first, count)],
            got.at[m, pl.ds(slot, count)],
            rs_send.at[i],
            recv.at[m],
            device_id=(mode, strip),
            device_id_type=MESH,
        )
        sends.append((c, when))
        if when is None:
            c.start()
        else:
            pl.when(when)(c.start)

    loads[0].wait()
    lax.fori_loop(0, 4, pass_one, 0)
    send(0, 2, 1, 3, left, 0, rs_recv, None)
    send(1, 3, 0, 1, s, 1, rs_recv, m != 1)
    send(0, 1, 2, 0, s, 2, own_recv, m != 0)
    loads[1].wait()
    lax.fori_loop(4, 8, pass_one, 0)
    send(6, 2, 0, 0, right, 3, rs_recv, None)
    send(4, 3, 0, 2, s, 4, rs_recv, m != 2)
    send(7, 1, 0, 3, s, 5, own_recv, m != 3)

    for owner, slot, first, count in ((0, 2, 0, 1), (1, 0, 1, 3), (2, 0, 4, 3), (3, 0, 7, 1)):
        @pl.when(m == owner)
        def _(owner=owner, slot=slot, first=first, count=count):
            got[owner, slot : slot + count] = part[first : first + count]

    for c in small[5:]:
        c.wait()

    warm, bend = pv[16:17, :], pv[24:25, :]
    own_warm, own_bend = own(warm), own(bend)
    tab[WARM_HALF] = 0.5 * own_warm / own_bend
    tab[CURVE] = own_bend * (1.0 / math.log(2.0))
    tab[HOT] = (0.5 * own_warm / own_bend) * (jnp.exp(own_bend * HOT_WALL) - jnp.exp(-own_bend * HOT_WALL))
    codes = own(oc[0:1, :].astype(F32)).astype(jnp.int32)
    tab[GO_X] = 1.0 - (codes & 1).astype(F32)
    tab[GO_Z] = 1.0 - (codes // 4).astype(F32)
    tab[X0], tab[X1], tab[X2] = sweep_factors(own(cx))
    tab[Y0], tab[Y1], tab[Y2] = sweep_factors(own(cy))
    tab[CZ] = own(cz)

    def weights(p, b, held, inverse):
        kept = jnp.exp(row(N_RATE, b) + row(N_SPEED, b) * inverse)
        uu[b, p] = kept * held
        ww[b, p] = (1.0 - kept) * row(WARM_HALF, b)

    def pass_two(r, carry):
        inverse = 1.0 / sp[2 + r]
        fluid = fl[r]
        for b in range(16):
            held = st[b, 2 + r] * fluid
            st[b, 2 + r] = held
            weights(2 + r, b, held, inverse)
        return carry

    lax.fori_loop(0, 8, pass_two, 0)

    halos = []
    for i, (src, dst, strip) in enumerate(((8, 0, right), (2, 10, left))):
        for j, (a, b) in enumerate(
            (
                (sp.at[pl.ds(src, 2)], sp.at[pl.ds(dst, 2)]),
                (st.at[:, pl.ds(src, 2)], st.at[:, pl.ds(dst, 2)]),
            )
        ):
            halos.append(
                pltpu.make_async_remote_copy(
                    a, b, h_send.at[2 * i + j], h_recv.at[2 * i + j], device_id=(m, strip), device_id_type=MESH
                )
            )

    @pl.when(early)
    def _():
        for c in halos:
            c.start()

    depth = lax.broadcasted_iota(jnp.int32, (16, 128), 0)

    def wall_rows(r, carry):
        low = jnp.broadcast_to(wl[0, pl.ds(r, 1), :], (16, 128))
        high = jnp.broadcast_to(wl[1, pl.ds(r, 1), :], (16, 128))
        up_keep[r] = jnp.where((depth == 15) & (high == 0), 0.0, 1.0)
        dn_keep[r] = jnp.where((depth == 0) & (low == 0), 0.0, 1.0)
        bot[r] = jnp.where((depth == 0) & (low == 2), 1.0, 0.0)
        top[r] = jnp.where((depth == 15) & (high == 2), 1.0, 0.0)
        return carry

    lax.fori_loop(0, 8, wall_rows, 0)

    def series():
        order = lax.broadcasted_iota(jnp.int32, (16, 128), 0)
        rest = jnp.exp(-rate)
        powers = jnp.zeros((16, 128), F32)
        term = -rest
        for j in range(RATE_TERMS):
            value = 1.0 - rest if j == 0 else term
            powers = jnp.where(order == j, jnp.broadcast_to(value, (16, 128)), powers)
            term = term * (-speed) * (1.0 / (j + 1))
        weight = warm
        for k in range(TERMS):
            summed = jnp.sum(powers * weight, axis=1, keepdims=True)
            zt[k] = jnp.broadcast_to(summed, (16, 128))
            weight = weight * (bend * bend) * (SCALE * SCALE / ((2 * k + 2) * (2 * k + 3)))

    def moments(p, i):
        inverse = 1.0 / sp[p]
        for k in range(TERMS):
            value = jnp.broadcast_to(zt[k, RATE_TERMS - 1 : RATE_TERMS, :], (16, 128))
            for j in range(RATE_TERMS - 2, -1, -1):
                value = value * inverse + zt[k, j : j + 1, :]
            mu[k, i] = value
        return None

    def iterations(base, slot, count, arrivals):
        for k, recv in arrivals:
            pltpu.make_async_remote_copy(
                part.at[pl.ds(0, count)], got.at[k, pl.ds(slot, count)], rs_send.at[0], recv.at[k],
                device_id=(m, s), device_id_type=MESH,
            ).wait_recv()
        rows = slice(slot, slot + count)
        total = got[0, rows]
        for k in range(1, 8):
            total = total + got[k, rows]
        t = RELAX_WEIGHT * total / mu[0, rows]

        def iterate(_, t):
            q = (t * (1.0 / SCALE)) * (t * (1.0 / SCALE))
            value = mu[TERMS - 1, rows]
            slope = value
            for k in range(TERMS - 2, -1, -1):
                value = value * q + mu[k, rows]
                if k > 0:
                    slope = slope * q + value
            return t - RELAX_WEIGHT * (t * value - total) / (value + 2.0 * q * slope)

        tp[base : base + count] = lax.fori_loop(1, ITERS, iterate, t)

    def t_copy(piece, mode, i):
        _, base, _, count, _ = PIECES[piece]
        return pltpu.make_async_remote_copy(
            tp.at[pl.ds(base, count)], tp.at[pl.ds(base, count)], t_send.at[i], t_recv.at[piece],
            device_id=(mode, s), device_id_type=MESH,
        )

    OWNED = {0: (0, 4), 1: (1,), 2: (2,), 3: (3, 5)}
    pl.when(early)(series)
    for owner in range(4):
        @pl.when(m == owner)
        def _(owner=owner):
            if owner == 0:
                halos[0].wait_recv()
            if owner == 3:
                halos[2].wait_recv()
            lax.fori_loop(0, 3, lambda i, carry: moments(3 * owner + i, i), None)
            for stage, piece in enumerate(OWNED[owner]):
                _, base, slot, count, strip_only = PIECES[piece]
                recv = own_recv if strip_only and count == 1 else rs_recv
                iterations(base, slot, count, [(k, recv) for k in range(8) if k != owner or not strip_only])
                for j in range(1, 4):
                    t_copy(piece, (owner + j) % 4, 8 * stage + j).start()
                if stage == 0:
                    pl.semaphore_wait(l_sem, 4)
                for j in range(4):
                    t_copy(piece, 4 + j, 8 * stage + 4 + j).start()

    @pl.when(late & trails)
    def _():
        for c in halos:
            c.start()

    @pl.when(late & leads)
    def _():
        pl.semaphore_wait(right_sem, 1)
        for c in halos[:2]:
            c.start()
        pl.semaphore_wait(left_sem, 1)
        for c in halos[2:]:
            c.start()

    @pl.when(late & ~leads & ~trails)
    def _():
        for c in halos[2:]:
            c.start()
        pl.semaphore_wait(right_sem, 1)
        for c in halos[:2]:
            c.start()

    def halo_rows(first):
        for p in (first, first + 1):
            inverse = 1.0 / sp[p]
            for b in range(16):
                weights(p, b, st[b, p], inverse)

    def halo_in():
        for i, c in enumerate(halos):
            if i == 0:
                pl.when(m != 0)(c.wait_recv)
            elif i == 2:
                pl.when(m != 3)(c.wait_recv)
            else:
                c.wait_recv()
                halo_rows((0, 10)[i // 2])

    def t_in(piece):
        owner = PIECES[piece][0]
        pl.when(m != owner)(t_copy(piece, owner, 0).wait_recv)

    pl.when(early)(halo_in)
    for piece in range(4):
        t_in(piece)

    def inner_across(b, carry):
        for p in range(2, 10):
            uu[b, p] = relaxed(tp[p], uu[b, p], ww[b, p], row(CURVE, b))
        cells = {p: uu[b, p] for p in range(2, 10)}
        across(b, row, cells, INNER, (up_keep, dn_keep, bot, top), state)
        return carry

    lax.fori_loop(0, 16, inner_across, 0)

    def inner_along(i, carry):
        for j in range(8):
            along(8 * i + j, row, octants[0, 16 * m + 8 * i + j], INNER, fl, state, res)
        return carry

    lax.fori_loop(0, 2, inner_along, 0)
    pl.when(late)(halo_in)
    t_in(4)
    t_in(5)

    for c, when in sends:
        if when is None:
            c.wait_send()
        else:
            pl.when(when)(c.wait_send)
    for c in halos:
        c.wait_send()
    for owner in range(4):
        @pl.when(m == owner)
        def _(owner=owner):
            for stage, piece in enumerate(OWNED[owner]):
                for j in range(1, 8):
                    t_copy(piece, owner, 8 * stage + j).wait_send()


def sweeps(uu, ww, tp, fl, up_keep, dn_keep, bot, top, tab, oc, inner, out, temp_out, state, res, octants, sems):
    signs = pltpu.make_async_copy(oc, octants, sems.at[0])
    signs.start()
    first, count = INNER[0], len(INNER)
    copies = [
        pltpu.make_async_copy(tp.at[pl.ds(2, 8)], temp_out, sems.at[1]),
        pltpu.make_async_copy(inner, out.at[:, pl.ds(first, count)], sems.at[2]),
    ]
    for c in copies:
        c.start()

    def row(table, b):
        return tab[table, pl.ds(b, 1), :]

    def outer_across(b, carry):
        go_x = jnp.broadcast_to(row(GO_X, b), (16, 128)) > 0.5
        cells = {p: uu[b, p] for p in range(2, 10)}
        for p, q in ((1, 10), (0, 11)):
            cells[p] = cells[q] = relaxed(
                jnp.where(go_x, tp[p], tp[q]),
                jnp.where(go_x, uu[b, p], uu[b, q]),
                jnp.where(go_x, ww[b, p], ww[b, q]),
                row(CURVE, b),
            )
        across(b, row, cells, OUTER, (up_keep, dn_keep, bot, top), state)
        return carry

    lax.fori_loop(0, 16, outer_across, 0)
    signs.wait()
    mode = lax.axis_index("mode")

    def outer_along(i, carry):
        for j in range(8):
            along(8 * i + j, row, octants[0, 16 * mode + 8 * i + j], OUTER, fl, state, res)
        for e in range(2):
            pltpu.make_async_copy(
                res.at[pl.ds(8 * i, 8), pl.ds(2 * e, 2)], out.at[pl.ds(8 * i, 8), pl.ds(6 * e, 2)], sems.at[3 + 2 * i + e]
            ).start()
        return carry

    for i in range(2):
        outer_along(i, None)
    for i in range(2):
        for e in range(2):
            copies.append(
                pltpu.make_async_copy(
                    res.at[pl.ds(8 * i, 8), pl.ds(2 * e, 2)], out.at[pl.ds(8 * i, 8), pl.ds(6 * e, 2)], sems.at[3 + 2 * i + e]
                )
            )
    for c in copies:
        c.wait()


def solution(mesh):
    space = mesh.shape["space"]

    def local(energy, void, spacing, walls, octant, warmth, curve, umklapp, isotope, courant):
        flat = lambda v: v.reshape(1, 128)
        vmem = pl.BlockSpec(memory_space=pltpu.VMEM)
        dma = pltpu.SemaphoreType.DMA
        regular = pltpu.SemaphoreType.REGULAR
        held, quarter = (16, 12, 16, 128), (16, 4, 16, 128)
        cells = spacing.shape
        sums = pl.pallas_call(
            functools.partial(kernel, space),
            out_shape=(
                [pltpu.VMEM(held, F32)] * 2
                + [pltpu.VMEM((12, 16, 128), F32)]
                + [pltpu.VMEM(cells, F32)] * 5
                + [pltpu.VMEM((14, 16, 128), F32), pltpu.VMEM((1, 128), jnp.int32), pltpu.VMEM(quarter, F32)]
            ),
            in_specs=[pl.BlockSpec(memory_space=pltpu.HBM)] * 10,
            out_specs=[vmem] * 11,
            scratch_shapes=[
                pltpu.VMEM(quarter, F32),
                pltpu.SMEM((1, 128), jnp.int32),
                pltpu.VMEM(held, F32),
                pltpu.VMEM((12, 16, 128), F32),
                pltpu.VMEM(cells, jnp.int32),
                pltpu.VMEM((2, 8, 128), jnp.int32),
                pltpu.VMEM((32, 128), F32),
                pltpu.VMEM((3, 128), F32),
                pltpu.VMEM(cells, F32),
                pltpu.VMEM((8, 3, 16, 128), F32),
                pltpu.VMEM((TERMS, 3, 16, 128), F32),
                pltpu.VMEM((TERMS, 16, 128), F32),
                dma((2,)),
                dma((10,)),
                dma((6,)),
                dma((8,)),
                dma((8,)),
                dma((16,)),
                dma((6,)),
                dma((4,)),
                dma((4,)),
                regular,
                regular,
                regular,
            ],
            compiler_params=pltpu.CompilerParams(
                collective_id=0, has_side_effects=True, vmem_limit_bytes=24 * 1024 * 1024
            ),
        )(
            *[
                pltpu.with_memory_space_constraint(v, pltpu.HBM)
                for v in (
                    energy, void, spacing, walls, flat(octant), flat(warmth), flat(curve), flat(umklapp),
                    flat(isotope), courant,
                )
            ]
        )
        return pl.pallas_call(
            sweeps,
            out_shape=(pltpu.HBM(energy.shape, F32), pltpu.HBM(cells, F32)),
            in_specs=[vmem] * 11,
            out_specs=[pl.BlockSpec(memory_space=pltpu.HBM)] * 2,
            scratch_shapes=[
                pltpu.VMEM(quarter, F32),
                pltpu.VMEM(quarter, F32),
                pltpu.SMEM((1, 128), jnp.int32),
                dma((7,)),
            ],
            compiler_params=pltpu.CompilerParams(vmem_limit_bytes=24 * 1024 * 1024),
        )(*sums)

    in_specs = (
        P("mode", "space", None, None),
        P("space", None, None),
        P("space", None, None),
        P(None, "space", None),
        P(),
        P(),
        P(),
        P(),
        P(),
        P(),
    )
    out_specs = (P("mode", "space", None, None), P("space", None, None))
    return jax.shard_map(local, mesh=mesh, in_specs=in_specs, out_specs=out_specs, check_vma=False)
```

```python
import functools
import math

import jax
import jax.numpy as jnp
from jax import lax
from jax.experimental import pallas as pl
from jax.experimental.pallas import tpu as pltpu
from jax.sharding import PartitionSpec as P

MESH = pl.DeviceIdType.MESH
ITERS = 8
RELAX_WEIGHT = 0.35
HOT_WALL = 1.0
RUN = 8
TERMS = 22
RATE_TERMS = 12
SCALE = 8.0
F32 = jnp.float32

(N_RATE, N_SPEED, WARM_HALF, CURVE, GO_X, GO_Z, X0, X1, X2, CZ, Y0, Y1, Y2, HOT) = range(14)


def sweep_factors(c):
    return 1.0 - 1.5 * c + 0.5 * c * c, 2.0 * c - c * c, 0.5 * c * c - 0.5 * c


OWNERS = (1, 2, 0, 3)
PIECES = ((0, 2, 2, 1, True), (1, 3, 0, 3, True), (2, 6, 0, 3, True), (3, 9, 0, 1, True), (0, 0, 0, 2, False), (3, 10, 1, 2, False))
INNER, OUTER = (2, 3, 4, 5), (0, 1, 6, 7)


def relaxed(t, held, pull, bend):
    x = t * bend
    return held + pull * (jnp.exp2(x) - jnp.exp2(-x))


def across(b, row, cells, rows, walls, state):
    up_keep, dn_keep, bot, top = walls
    depth = lax.broadcasted_iota(jnp.int32, (16, 128), 0)
    go_x = jnp.broadcast_to(row(GO_X, b), (16, 128)) > 0.5
    go_z = jnp.broadcast_to(row(GO_Z, b), (16, 128)) > 0.5
    inflow = jnp.where(go_z, depth, 15 - depth) == 0
    for i, r in enumerate(rows):
        p = r + 2
        near = jnp.where(go_x, cells[p - 1], cells[p + 1])
        far = jnp.where(go_x, cells[p - 2], cells[p + 2])
        a = row(X0, b) * cells[p] + row(X1, b) * near + row(X2, b) * far
        up = jnp.where(go_z, pltpu.roll(a, 1, 0), pltpu.roll(a, 15, 0))
        up = jnp.where(inflow, jnp.where(go_z, bot[r], top[r]) * row(HOT, b), up)
        keep = jnp.where(go_z, up_keep[r], dn_keep[r])
        state[b, i] = a + row(CZ, b) * (up - keep * a)


def along(b, row, octant, rows, fl, state, res):
    shift = jnp.where((octant & 2) == 0, 1, 127)
    twice = jnp.where((octant & 2) == 0, 2, 126)
    for i, r in enumerate(rows):
        a = state[b, i]
        near, far = pltpu.roll(a, shift, 1), pltpu.roll(a, twice, 1)
        res[b, i] = (row(Y0, b) * a + row(Y1, b) * near + row(Y2, b) * far) * fl[r]


def kernel(
    space,
    energy, void, spacing, walls, octant, warmth, curve, umklapp, isotope, courant,
    uu, ww, tp, fl, up_keep, dn_keep, bot, top, tab, oc, res,
    state, octants, st, sp, vd, wl, pv, cr, part, got, mu, mu_slope, zt,
    in_sem, small_sem, rs_send, rs_recv, own_recv, t_send, t_recv, h_send, h_recv, l_sem, left_sem, right_sem,
):
    m, s = lax.axis_index("mode"), lax.axis_index("space")
    left, right = lax.rem(s + space - 1, space), lax.rem(s + 1, space)
    y = lax.rem(m, 4)
    early = m < 4
    late = m >= 4

    def signal(sem, mode, strip):
        pl.semaphore_signal(sem, inc=1, device_id=(mode, strip), device_id_type=MESH)

    barrier = pltpu.get_barrier_semaphore()

    @pl.when(early)
    def _():
        for j in range(4):
            signal(barrier, 4 + j, s)

    @pl.when(m == OWNERS[0])
    def _():
        for k in range(8):
            signal(barrier, 7 - k, left)

    @pl.when(m == OWNERS[3])
    def _():
        for k in range(8):
            signal(barrier, 7 - k, right)

    @pl.when(early)
    def _():
        for j in range(1, 4):
            signal(barrier, lax.rem(m + j, 4), s)
        for strip in (left, right):
            signal(barrier, y, strip)

    small = [
        pltpu.make_async_copy(src, dst, small_sem.at[i])
        for i, (src, dst) in enumerate(
            (
                (spacing, sp.at[pl.ds(2, 8)]),
                (void, vd),
                (umklapp, pv.at[pl.ds(0, 1)]),
                (isotope, pv.at[pl.ds(8, 1)]),
                (courant, cr),
                (warmth, pv.at[pl.ds(16, 1)]),
                (curve, pv.at[pl.ds(24, 1)]),
                (octant, oc),
                (walls, wl),
                (octant, octants),
            )
        )
    ]
    loads = [
        pltpu.make_async_copy(
            energy.at[:, pl.ds(4 * i, 4)], st.at[:, pl.ds(2 + 4 * i, 4)], in_sem.at[i]
        )
        for i in range(2)
    ]
    for c in small[:5]:
        c.start()
    for c in loads:
        c.start()
    for c in small[5:]:
        c.start()

    place = lax.rem(s, RUN)
    leads, trails = place == 0, place == RUN - 1

    @pl.when(late & ~trails)
    def _():
        signal(barrier, m, right)

    @pl.when(late & leads)
    def _():
        signal(barrier, m, left)

    for c in small[:5]:
        c.wait()

    lane = lax.broadcasted_iota(jnp.int32, (16, 128), 1)
    band = lax.broadcasted_iota(jnp.int32, (16, 128), 0) + 16 * m

    def own(vector):
        picked = jnp.where(lane == band, jnp.broadcast_to(vector, (16, 128)), 0.0)
        return jnp.broadcast_to(jnp.sum(picked, axis=1, keepdims=True), (16, 128))

    rate = pv[0:1, :] + pv[8:9, :]
    cx, cy, cz = cr[0:1, :], cr[1:2, :], cr[2:3, :]
    speed = jnp.sqrt(cx * cx + cy * cy + cz * cz)
    tab[N_RATE] = own(-rate)
    tab[N_SPEED] = own(-speed)

    def row(table, b):
        return tab[table, pl.ds(b, 1), :]

    def pass_one(r, carry):
        inverse = 1.0 / sp[2 + r]
        total = jnp.zeros((16, 128), F32)
        for b in range(16):
            kept = jnp.exp(row(N_RATE, b) + row(N_SPEED, b) * inverse)
            total = total + (1.0 - kept) * st[b, 2 + r]
        fluid = (1 - vd[r]).astype(F32)
        fl[r] = fluid
        part[r] = total * fluid
        return carry

    sends = []

    def send(first, count, slot, mode, strip, i, recv, when):
        c = pltpu.make_async_remote_copy(
            part.at[pl.ds(first, count)],
            got.at[m, pl.ds(slot, count)],
            rs_send.at[i],
            recv.at[m],
            device_id=(mode, strip),
            device_id_type=MESH,
        )
        sends.append((c, when))
        if when is None:
            c.start()
        else:
            pl.when(when)(c.start)

    for i in range(2):
        loads[i].wait()
        lax.fori_loop(4 * i, 4 * i + 4, pass_one, 0)

    pl.semaphore_wait(barrier, jnp.where(early, 7, 7 + trails.astype(jnp.int32) - leads.astype(jnp.int32)))
    send(6, 2, 0, OWNERS[0], right, 3, rs_recv, None)
    send(0, 2, 1, OWNERS[3], left, 0, rs_recv, None)
    send(1, 3, 0, OWNERS[1], s, 1, rs_recv, m != OWNERS[1])
    send(4, 3, 0, OWNERS[2], s, 4, rs_recv, m != OWNERS[2])
    send(0, 1, 2, OWNERS[0], s, 2, own_recv, m != OWNERS[0])
    send(7, 1, 0, OWNERS[3], s, 5, own_recv, m != OWNERS[3])

    @pl.when(late)
    def _():
        for k in range(4):
            signal(l_sem, k, s)

    @pl.when(late & ~leads)
    def _():
        signal(right_sem, m, left)

    @pl.when(late & trails)
    def _():
        signal(left_sem, m, right)

    for role, slot, first, count in ((0, 2, 0, 1), (1, 0, 1, 3), (2, 0, 4, 3), (3, 0, 7, 1)):
        owner = OWNERS[role]

        @pl.when(m == owner)
        def _(owner=owner, slot=slot, first=first, count=count):
            got[owner, slot : slot + count] = part[first : first + count]

    for c in small[5:]:
        c.wait()

    warm, bend = pv[16:17, :], pv[24:25, :]
    own_warm, own_bend = own(warm), own(bend)
    tab[WARM_HALF] = 0.5 * own_warm / own_bend
    tab[CURVE] = own_bend * (1.0 / math.log(2.0))
    tab[HOT] = (0.5 * own_warm / own_bend) * (jnp.exp(own_bend * HOT_WALL) - jnp.exp(-own_bend * HOT_WALL))
    codes = own(oc[0:1, :].astype(F32)).astype(jnp.int32)
    tab[GO_X] = 1.0 - (codes & 1).astype(F32)
    tab[GO_Z] = 1.0 - (codes // 4).astype(F32)
    tab[X0], tab[X1], tab[X2] = sweep_factors(own(cx))
    tab[Y0], tab[Y1], tab[Y2] = sweep_factors(own(cy))
    tab[CZ] = own(cz)

    def weights(p, b, held, inverse):
        kept = jnp.exp(row(N_RATE, b) + row(N_SPEED, b) * inverse)
        uu[b, p] = kept * held
        ww[b, p] = (1.0 - kept) * row(WARM_HALF, b)

    def pass_two(r, carry):
        inverse = 1.0 / sp[2 + r]
        fluid = fl[r]
        for b in range(16):
            held = st[b, 2 + r] * fluid
            st[b, 2 + r] = held
            weights(2 + r, b, held, inverse)
        return carry

    lax.fori_loop(0, 8, pass_two, 0)

    halos = []
    for i, (src, dst, strip) in enumerate(((8, 0, right), (2, 10, left))):
        for j, (a, b) in enumerate(
            (
                (sp.at[pl.ds(src, 2)], sp.at[pl.ds(dst, 2)]),
                (st.at[:, pl.ds(src, 2)], st.at[:, pl.ds(dst, 2)]),
            )
        ):
            halos.append(
                pltpu.make_async_remote_copy(
                    a, b, h_send.at[2 * i + j], h_recv.at[2 * i + j], device_id=(m, strip), device_id_type=MESH
                )
            )

    @pl.when(early)
    def _():
        for c in halos:
            c.start()

    depth = lax.broadcasted_iota(jnp.int32, (16, 128), 0)

    def wall_rows(r, carry):
        low = jnp.broadcast_to(wl[0, pl.ds(r, 1), :], (16, 128))
        high = jnp.broadcast_to(wl[1, pl.ds(r, 1), :], (16, 128))
        up_keep[r] = jnp.where((depth == 15) & (high == 0), 0.0, 1.0)
        dn_keep[r] = jnp.where((depth == 0) & (low == 0), 0.0, 1.0)
        bot[r] = jnp.where((depth == 0) & (low == 2), 1.0, 0.0)
        top[r] = jnp.where((depth == 15) & (high == 2), 1.0, 0.0)
        return carry

    lax.fori_loop(0, 8, wall_rows, 0)

    def series():
        order = lax.broadcasted_iota(jnp.int32, (16, 128), 0)
        rest = jnp.exp(-rate)
        powers = jnp.zeros((16, 128), F32)
        term = -rest
        for j in range(RATE_TERMS):
            value = 1.0 - rest if j == 0 else term
            powers = jnp.where(order == j, jnp.broadcast_to(value, (16, 128)), powers)
            term = term * (-speed) * (1.0 / (j + 1))
        weight = warm
        for k in range(TERMS):
            summed = jnp.sum(powers * weight, axis=1, keepdims=True)
            zt[k] = jnp.broadcast_to(summed, (16, 128))
            weight = weight * (bend * bend) * (SCALE * SCALE / ((2 * k + 2) * (2 * k + 3)))

    def moments(p, i):
        inverse = 1.0 / sp[p]
        for k in range(TERMS):
            value = jnp.broadcast_to(zt[k, RATE_TERMS - 1 : RATE_TERMS, :], (16, 128))
            for j in range(RATE_TERMS - 2, -1, -1):
                value = value * inverse + zt[k, j : j + 1, :]
            mu[k, i] = value
            mu_slope[k, i] = value * (2.0 * k + 1.0)
        return None

    def iterations(base, slot, count, arrivals):
        for k, recv in arrivals:
            pltpu.make_async_remote_copy(
                part.at[pl.ds(0, count)], got.at[k, pl.ds(slot, count)], rs_send.at[0], recv.at[k],
                device_id=(m, s), device_id_type=MESH,
            ).wait_recv()
        rows = slice(slot, slot + count)
        total = got[0, rows]
        for k in range(1, 8):
            total = total + got[k, rows]
        t = RELAX_WEIGHT * total / mu[0, rows]

        def iterate(_, t):
            q = (t * (1.0 / SCALE)) * (t * (1.0 / SCALE))
            square = q * q

            def series_at(table):
                even, odd = table[TERMS - 2, rows], table[TERMS - 1, rows]
                for k in range(TERMS - 4, -1, -2):
                    even = even * square + table[k, rows]
                    odd = odd * square + table[k + 1, rows]
                return even + q * odd

            return t - RELAX_WEIGHT * (t * series_at(mu) - total) / series_at(mu_slope)

        tp[base : base + count] = lax.fori_loop(1, ITERS, iterate, t)

    def t_copy(piece, mode, i):
        _, base, _, count, _ = PIECES[piece]
        return pltpu.make_async_remote_copy(
            tp.at[pl.ds(base, count)], tp.at[pl.ds(base, count)], t_send.at[i], t_recv.at[piece],
            device_id=(mode, s), device_id_type=MESH,
        )

    OWNED = {0: (0, 4), 1: (1,), 2: (2,), 3: (3, 5)}
    pl.when(early)(series)
    for role, owner in enumerate(OWNERS):
        @pl.when(m == owner)
        def _(role=role, owner=owner):
            if role == 0:
                halos[0].wait_recv()
            if role == 3:
                halos[2].wait_recv()
            lax.fori_loop(0, 3, lambda i, carry: moments(3 * role + i, i), None)
            for stage, piece in enumerate(OWNED[role]):
                _, base, slot, count, strip_only = PIECES[piece]
                recv = own_recv if strip_only and count == 1 else rs_recv
                iterations(base, slot, count, [(k, recv) for k in range(8) if k != owner or not strip_only])
                for j in range(1, 4):
                    t_copy(piece, (owner + j) % 4, 8 * stage + j).start()
                if stage == 0:
                    pl.semaphore_wait(l_sem, 4)
                for j in range(4):
                    t_copy(piece, 4 + j, 8 * stage + 4 + j).start()

    @pl.when(late & trails)
    def _():
        for c in halos:
            c.start()

    @pl.when(late & leads)
    def _():
        pl.semaphore_wait(right_sem, 1)
        for c in halos[:2]:
            c.start()
        pl.semaphore_wait(left_sem, 1)
        for c in halos[2:]:
            c.start()

    @pl.when(late & ~leads & ~trails)
    def _():
        for c in halos[2:]:
            c.start()
        pl.semaphore_wait(right_sem, 1)
        for c in halos[:2]:
            c.start()

    def halo_rows(first):
        for p in (first, first + 1):
            inverse = 1.0 / sp[p]
            for b in range(16):
                weights(p, b, st[b, p], inverse)

    def halo_in():
        for i, c in enumerate(halos):
            if i == 0:
                pl.when(m != OWNERS[0])(c.wait_recv)
            elif i == 2:
                pl.when(m != OWNERS[3])(c.wait_recv)
            else:
                c.wait_recv()
                halo_rows((0, 10)[i // 2])

    def t_in(piece):
        owner = OWNERS[PIECES[piece][0]]
        pl.when(m != owner)(t_copy(piece, owner, 0).wait_recv)

    pl.when(early)(halo_in)
    for piece in range(4):
        t_in(piece)

    def inner_across(b, carry):
        for p in range(2, 10):
            uu[b, p] = relaxed(tp[p], uu[b, p], ww[b, p], row(CURVE, b))
        cells = {p: uu[b, p] for p in range(2, 10)}
        across(b, row, cells, INNER, (up_keep, dn_keep, bot, top), state)
        return carry

    lax.fori_loop(0, 16, inner_across, 0)

    def inner_along(i, carry):
        for j in range(8):
            along(8 * i + j, row, octants[0, 16 * m + 8 * i + j], INNER, fl, state, res)
        return carry

    lax.fori_loop(0, 2, inner_along, 0)
    pl.when(late)(halo_in)
    t_in(4)
    t_in(5)

    for c, when in sends:
        if when is None:
            c.wait_send()
        else:
            pl.when(when)(c.wait_send)
    for c in halos:
        c.wait_send()
    for role, owner in enumerate(OWNERS):
        @pl.when(m == owner)
        def _(role=role, owner=owner):
            for stage, piece in enumerate(OWNED[role]):
                for j in range(1, 8):
                    t_copy(piece, owner, 8 * stage + j).wait_send()


def sweeps(uu, ww, tp, fl, up_keep, dn_keep, bot, top, tab, oc, inner, out, temp_out, state, res, octants, sems):
    signs = pltpu.make_async_copy(oc, octants, sems.at[0])
    signs.start()
    first, count = INNER[0], len(INNER)
    copies = [
        pltpu.make_async_copy(tp.at[pl.ds(2, 8)], temp_out, sems.at[1]),
        pltpu.make_async_copy(inner, out.at[:, pl.ds(first, count)], sems.at[2]),
    ]
    for c in copies:
        c.start()

    def row(table, b):
        return tab[table, pl.ds(b, 1), :]

    def outer_across(b, carry):
        go_x = jnp.broadcast_to(row(GO_X, b), (16, 128)) > 0.5
        cells = {p: uu[b, p] for p in range(2, 10)}
        for p, q in ((1, 10), (0, 11)):
            cells[p] = cells[q] = relaxed(
                jnp.where(go_x, tp[p], tp[q]),
                jnp.where(go_x, uu[b, p], uu[b, q]),
                jnp.where(go_x, ww[b, p], ww[b, q]),
                row(CURVE, b),
            )
        across(b, row, cells, OUTER, (up_keep, dn_keep, bot, top), state)
        return carry

    lax.fori_loop(0, 16, outer_across, 0)
    signs.wait()
    mode = lax.axis_index("mode")

    def outer_along(i, carry):
        for j in range(8):
            along(8 * i + j, row, octants[0, 16 * mode + 8 * i + j], OUTER, fl, state, res)
        for e in range(2):
            pltpu.make_async_copy(
                res.at[pl.ds(8 * i, 8), pl.ds(2 * e, 2)], out.at[pl.ds(8 * i, 8), pl.ds(6 * e, 2)], sems.at[3 + 2 * i + e]
            ).start()
        return carry

    for i in range(2):
        outer_along(i, None)
    for i in range(2):
        for e in range(2):
            copies.append(
                pltpu.make_async_copy(
                    res.at[pl.ds(8 * i, 8), pl.ds(2 * e, 2)], out.at[pl.ds(8 * i, 8), pl.ds(6 * e, 2)], sems.at[3 + 2 * i + e]
                )
            )
    for c in copies:
        c.wait()


def solution(mesh):
    space = mesh.shape["space"]

    def local(energy, void, spacing, walls, octant, warmth, curve, umklapp, isotope, courant):
        flat = lambda v: v.reshape(1, 128)
        vmem = pl.BlockSpec(memory_space=pltpu.VMEM)
        dma = pltpu.SemaphoreType.DMA
        regular = pltpu.SemaphoreType.REGULAR
        held, quarter = (16, 12, 16, 128), (16, 4, 16, 128)
        cells = spacing.shape
        sums = pl.pallas_call(
            functools.partial(kernel, space),
            out_shape=(
                [pltpu.VMEM(held, F32)] * 2
                + [pltpu.VMEM((12, 16, 128), F32)]
                + [pltpu.VMEM(cells, F32)] * 5
                + [pltpu.VMEM((14, 16, 128), F32), pltpu.VMEM((1, 128), jnp.int32), pltpu.VMEM(quarter, F32)]
            ),
            in_specs=[pl.BlockSpec(memory_space=pltpu.HBM)] * 10,
            out_specs=[vmem] * 11,
            scratch_shapes=[
                pltpu.VMEM(quarter, F32),
                pltpu.SMEM((1, 128), jnp.int32),
                pltpu.VMEM(held, F32),
                pltpu.VMEM((12, 16, 128), F32),
                pltpu.VMEM(cells, jnp.int32),
                pltpu.VMEM((2, 8, 128), jnp.int32),
                pltpu.VMEM((32, 128), F32),
                pltpu.VMEM((3, 128), F32),
                pltpu.VMEM(cells, F32),
                pltpu.VMEM((8, 3, 16, 128), F32),
                pltpu.VMEM((TERMS, 3, 16, 128), F32),
                pltpu.VMEM((TERMS, 3, 16, 128), F32),
                pltpu.VMEM((TERMS, 16, 128), F32),
                dma((2,)),
                dma((10,)),
                dma((6,)),
                dma((8,)),
                dma((8,)),
                dma((16,)),
                dma((6,)),
                dma((4,)),
                dma((4,)),
                regular,
                regular,
                regular,
            ],
            compiler_params=pltpu.CompilerParams(
                collective_id=0, has_side_effects=True, vmem_limit_bytes=24 * 1024 * 1024
            ),
        )(
            *[
                pltpu.with_memory_space_constraint(v, pltpu.HBM)
                for v in (
                    energy, void, spacing, walls, flat(octant), flat(warmth), flat(curve), flat(umklapp),
                    flat(isotope), courant,
                )
            ]
        )
        return pl.pallas_call(
            sweeps,
            out_shape=(pltpu.HBM(energy.shape, F32), pltpu.HBM(cells, F32)),
            in_specs=[vmem] * 11,
            out_specs=[pl.BlockSpec(memory_space=pltpu.HBM)] * 2,
            scratch_shapes=[
                pltpu.VMEM(quarter, F32),
                pltpu.VMEM(quarter, F32),
                pltpu.SMEM((1, 128), jnp.int32),
                dma((7,)),
            ],
            compiler_params=pltpu.CompilerParams(vmem_limit_bytes=24 * 1024 * 1024),
        )(*sums)

    in_specs = (
        P("mode", "space", None, None),
        P("space", None, None),
        P("space", None, None),
        P(None, "space", None),
        P(),
        P(),
        P(),
        P(),
        P(),
        P(),
    )
    out_specs = (P("mode", "space", None, None), P("space", None, None))
    return jax.shard_map(local, mesh=mesh, in_specs=in_specs, out_specs=out_specs, check_vma=False)
```

```python
import functools
import math

import jax
import jax.numpy as jnp
from jax import lax
from jax.experimental import pallas as pl
from jax.experimental.pallas import tpu as pltpu
from jax.sharding import PartitionSpec as P

MESH = pl.DeviceIdType.MESH
ITERS = 8
RELAX_WEIGHT = 0.35
HOT_WALL = 1.0
RUN = 8
TERMS = 22
RATE_TERMS = 12
SCALE = 8.0
F32 = jnp.float32

(N_RATE, N_SPEED, WARM_HALF, CURVE, GO_X, GO_Z, X0, X1, X2, CZ, Y0, Y1, Y2, HOT) = range(14)


def sweep_factors(c):
    return 1.0 - 1.5 * c + 0.5 * c * c, 2.0 * c - c * c, 0.5 * c * c - 0.5 * c


OWNERS = (1, 2, 0, 3)
PIECES = ((0, 2, 2, 1, True), (1, 3, 0, 3, True), (2, 6, 0, 3, True), (3, 9, 0, 1, True), (0, 0, 0, 2, False), (3, 10, 1, 2, False))
INNER, OUTER = (2, 3, 4, 5), (0, 1, 6, 7)


def relaxed(t, held, pull, bend):
    x = t * bend
    return held + pull * (jnp.exp2(x) - jnp.exp2(-x))


def across(b, row, cells, rows, walls, state):
    up_keep, dn_keep, bot, top = walls
    depth = lax.broadcasted_iota(jnp.int32, (16, 128), 0)
    go_x = jnp.broadcast_to(row(GO_X, b), (16, 128)) > 0.5
    go_z = jnp.broadcast_to(row(GO_Z, b), (16, 128)) > 0.5
    inflow = jnp.where(go_z, depth, 15 - depth) == 0
    for i, r in enumerate(rows):
        p = r + 2
        near = jnp.where(go_x, cells[p - 1], cells[p + 1])
        far = jnp.where(go_x, cells[p - 2], cells[p + 2])
        a = row(X0, b) * cells[p] + row(X1, b) * near + row(X2, b) * far
        up = jnp.where(go_z, pltpu.roll(a, 1, 0), pltpu.roll(a, 15, 0))
        up = jnp.where(inflow, jnp.where(go_z, bot[r], top[r]) * row(HOT, b), up)
        keep = jnp.where(go_z, up_keep[r], dn_keep[r])
        state[b, i] = a + row(CZ, b) * (up - keep * a)


def along(b, row, octant, rows, fl, state, res):
    shift = jnp.where((octant & 2) == 0, 1, 127)
    twice = jnp.where((octant & 2) == 0, 2, 126)
    for i, r in enumerate(rows):
        a = state[b, i]
        near, far = pltpu.roll(a, shift, 1), pltpu.roll(a, twice, 1)
        res[b, i] = (row(Y0, b) * a + row(Y1, b) * near + row(Y2, b) * far) * fl[r]


def kernel(
    space,
    energy, void, spacing, walls, octant, warmth, curve, umklapp, isotope, courant,
    uu, ww, tp, fl, up_keep, dn_keep, bot, top, tab, oc, res,
    state, octants, st, sp, vd, wl, pv, cr, part, got, mu, mu_slope, zt,
    in_sem, small_sem, rs_send, rs_recv, own_recv, t_send, t_recv, h_send, h_recv, l_sem, left_sem, right_sem,
):
    m, s = lax.axis_index("mode"), lax.axis_index("space")
    left, right = lax.rem(s + space - 1, space), lax.rem(s + 1, space)
    y = lax.rem(m, 4)
    early = m < 4
    late = m >= 4

    def signal(sem, mode, strip):
        pl.semaphore_signal(sem, inc=1, device_id=(mode, strip), device_id_type=MESH)

    barrier = pltpu.get_barrier_semaphore()

    @pl.when(early)
    def _():
        for j in range(4):
            signal(barrier, 4 + j, s)

    @pl.when(m == OWNERS[0])
    def _():
        for k in range(8):
            signal(barrier, 7 - k, left)

    @pl.when(m == OWNERS[3])
    def _():
        for k in range(8):
            signal(barrier, 7 - k, right)

    @pl.when(early)
    def _():
        for j in range(1, 4):
            signal(barrier, lax.rem(m + j, 4), s)
        for strip in (left, right):
            signal(barrier, y, strip)

    small = [
        pltpu.make_async_copy(src, dst, small_sem.at[i])
        for i, (src, dst) in enumerate(
            (
                (spacing, sp.at[pl.ds(2, 8)]),
                (void, vd),
                (umklapp, pv.at[pl.ds(0, 1)]),
                (isotope, pv.at[pl.ds(8, 1)]),
                (courant, cr),
                (warmth, pv.at[pl.ds(16, 1)]),
                (curve, pv.at[pl.ds(24, 1)]),
                (octant, oc),
                (walls, wl),
                (octant, octants),
            )
        )
    ]
    loads = [
        pltpu.make_async_copy(
            energy.at[:, pl.ds(4 * i, 4)], st.at[:, pl.ds(2 + 4 * i, 4)], in_sem.at[i]
        )
        for i in range(2)
    ]
    for c in small[:5]:
        c.start()
    for c in loads:
        c.start()
    for c in small[5:]:
        c.start()

    place = lax.rem(s, RUN)
    leads, trails = place == 0, place == RUN - 1

    @pl.when(late & ~trails)
    def _():
        signal(barrier, m, right)

    @pl.when(late & leads)
    def _():
        signal(barrier, m, left)

    for c in small[:5]:
        c.wait()

    lane = lax.broadcasted_iota(jnp.int32, (16, 128), 1)
    band = lax.broadcasted_iota(jnp.int32, (16, 128), 0) + 16 * m

    def own(vector):
        picked = jnp.where(lane == band, jnp.broadcast_to(vector, (16, 128)), 0.0)
        return jnp.broadcast_to(jnp.sum(picked, axis=1, keepdims=True), (16, 128))

    rate = pv[0:1, :] + pv[8:9, :]
    cx, cy, cz = cr[0:1, :], cr[1:2, :], cr[2:3, :]
    speed = jnp.sqrt(cx * cx + cy * cy + cz * cz)
    tab[N_RATE] = own(-rate)
    tab[N_SPEED] = own(-speed)

    def row(table, b):
        return tab[table, pl.ds(b, 1), :]

    def pass_one(r, carry):
        inverse = 1.0 / sp[2 + r]
        total = jnp.zeros((16, 128), F32)
        for b in range(16):
            kept = jnp.exp(row(N_RATE, b) + row(N_SPEED, b) * inverse)
            total = total + (1.0 - kept) * st[b, 2 + r]
        fluid = (1 - vd[r]).astype(F32)
        fl[r] = fluid
        part[r] = total * fluid
        return carry

    sends = []

    def send(first, count, slot, mode, strip, i, recv, when):
        c = pltpu.make_async_remote_copy(
            part.at[pl.ds(first, count)],
            got.at[m, pl.ds(slot, count)],
            rs_send.at[i],
            recv.at[m],
            device_id=(mode, strip),
            device_id_type=MESH,
        )
        sends.append((c, when))
        if when is None:
            c.start()
        else:
            pl.when(when)(c.start)

    for i in range(2):
        loads[i].wait()
        lax.fori_loop(4 * i, 4 * i + 4, pass_one, 0)

    pl.semaphore_wait(barrier, jnp.where(early, 7, 7 + trails.astype(jnp.int32) - leads.astype(jnp.int32)))
    send(6, 2, 0, OWNERS[0], right, 3, rs_recv, None)
    send(0, 2, 1, OWNERS[3], left, 0, rs_recv, None)
    send(1, 3, 0, OWNERS[1], s, 1, rs_recv, m != OWNERS[1])
    send(4, 3, 0, OWNERS[2], s, 4, rs_recv, m != OWNERS[2])
    send(0, 1, 2, OWNERS[0], s, 2, own_recv, m != OWNERS[0])
    send(7, 1, 0, OWNERS[3], s, 5, own_recv, m != OWNERS[3])

    @pl.when(late)
    def _():
        for k in range(4):
            signal(l_sem, k, s)

    @pl.when(late & ~leads)
    def _():
        signal(right_sem, m, left)

    @pl.when(late & trails)
    def _():
        signal(left_sem, m, right)

    def edges(b, carry):
        for r in OUTER:
            st[b, 2 + r] = st[b, 2 + r] * fl[r]
        return carry

    lax.fori_loop(0, 16, edges, 0)

    halos = []
    for i, (src, dst, strip) in enumerate(((8, 0, right), (2, 10, left))):
        for j, (a, b) in enumerate(
            (
                (sp.at[pl.ds(src, 2)], sp.at[pl.ds(dst, 2)]),
                (st.at[:, pl.ds(src, 2)], st.at[:, pl.ds(dst, 2)]),
            )
        ):
            halos.append(
                pltpu.make_async_remote_copy(
                    a, b, h_send.at[2 * i + j], h_recv.at[2 * i + j], device_id=(m, strip), device_id_type=MESH
                )
            )

    @pl.when(early | trails)
    def _():
        for c in halos[:2]:
            c.start()

    @pl.when(early | ~leads)
    def _():
        for c in halos[2:]:
            c.start()

    for role, slot, first, count in ((0, 2, 0, 1), (1, 0, 1, 3), (2, 0, 4, 3), (3, 0, 7, 1)):
        owner = OWNERS[role]

        @pl.when(m == owner)
        def _(owner=owner, slot=slot, first=first, count=count):
            got[owner, slot : slot + count] = part[first : first + count]

    for c in small[5:]:
        c.wait()

    warm, bend = pv[16:17, :], pv[24:25, :]
    own_warm, own_bend = own(warm), own(bend)
    tab[WARM_HALF] = 0.5 * own_warm / own_bend
    tab[CURVE] = own_bend * (1.0 / math.log(2.0))
    tab[HOT] = (0.5 * own_warm / own_bend) * (jnp.exp(own_bend * HOT_WALL) - jnp.exp(-own_bend * HOT_WALL))
    codes = own(oc[0:1, :].astype(F32)).astype(jnp.int32)
    tab[GO_X] = 1.0 - (codes & 1).astype(F32)
    tab[GO_Z] = 1.0 - (codes // 4).astype(F32)
    tab[X0], tab[X1], tab[X2] = sweep_factors(own(cx))
    tab[Y0], tab[Y1], tab[Y2] = sweep_factors(own(cy))
    tab[CZ] = own(cz)

    def weights(p, b, held, inverse):
        kept = jnp.exp(row(N_RATE, b) + row(N_SPEED, b) * inverse)
        uu[b, p] = kept * held
        ww[b, p] = (1.0 - kept) * row(WARM_HALF, b)

    def pass_two(r, carry):
        inverse = 1.0 / sp[2 + r]
        fluid = fl[r]
        for b in range(16):
            weights(2 + r, b, st[b, 2 + r] * fluid, inverse)
        return carry

    lax.fori_loop(0, 8, pass_two, 0)

    depth = lax.broadcasted_iota(jnp.int32, (16, 128), 0)

    def wall_rows(r, carry):
        low = jnp.broadcast_to(wl[0, pl.ds(r, 1), :], (16, 128))
        high = jnp.broadcast_to(wl[1, pl.ds(r, 1), :], (16, 128))
        up_keep[r] = jnp.where((depth == 15) & (high == 0), 0.0, 1.0)
        dn_keep[r] = jnp.where((depth == 0) & (low == 0), 0.0, 1.0)
        bot[r] = jnp.where((depth == 0) & (low == 2), 1.0, 0.0)
        top[r] = jnp.where((depth == 15) & (high == 2), 1.0, 0.0)
        return carry

    lax.fori_loop(0, 8, wall_rows, 0)

    def series():
        order = lax.broadcasted_iota(jnp.int32, (16, 128), 0)
        rest = jnp.exp(-rate)
        powers = jnp.zeros((16, 128), F32)
        term = -rest
        for j in range(RATE_TERMS):
            value = 1.0 - rest if j == 0 else term
            powers = jnp.where(order == j, jnp.broadcast_to(value, (16, 128)), powers)
            term = term * (-speed) * (1.0 / (j + 1))
        weight = warm
        for k in range(TERMS):
            summed = jnp.sum(powers * weight, axis=1, keepdims=True)
            zt[k] = jnp.broadcast_to(summed, (16, 128))
            weight = weight * (bend * bend) * (SCALE * SCALE / ((2 * k + 2) * (2 * k + 3)))

    def moments(p, i):
        inverse = 1.0 / sp[p]
        for k in range(TERMS):
            value = jnp.broadcast_to(zt[k, RATE_TERMS - 1 : RATE_TERMS, :], (16, 128))
            for j in range(RATE_TERMS - 2, -1, -1):
                value = value * inverse + zt[k, j : j + 1, :]
            mu[k, i] = value
            mu_slope[k, i] = value * (2.0 * k + 1.0)
        return None

    def iterations(base, slot, count, arrivals):
        for k, recv in arrivals:
            pltpu.make_async_remote_copy(
                part.at[pl.ds(0, count)], got.at[k, pl.ds(slot, count)], rs_send.at[0], recv.at[k],
                device_id=(m, s), device_id_type=MESH,
            ).wait_recv()
        rows = slice(slot, slot + count)
        total = got[0, rows]
        for k in range(1, 8):
            total = total + got[k, rows]
        t = RELAX_WEIGHT * total / mu[0, rows]

        def iterate(_, t):
            q = (t * (1.0 / SCALE)) * (t * (1.0 / SCALE))
            square = q * q

            def series_at(table):
                even, odd = table[TERMS - 2, rows], table[TERMS - 1, rows]
                for k in range(TERMS - 4, -1, -2):
                    even = even * square + table[k, rows]
                    odd = odd * square + table[k + 1, rows]
                return even + q * odd

            return t - RELAX_WEIGHT * (t * series_at(mu) - total) / series_at(mu_slope)

        tp[base : base + count] = lax.fori_loop(1, ITERS, iterate, t)

    def t_copy(piece, mode, i):
        _, base, _, count, _ = PIECES[piece]
        return pltpu.make_async_remote_copy(
            tp.at[pl.ds(base, count)], tp.at[pl.ds(base, count)], t_send.at[i], t_recv.at[piece],
            device_id=(mode, s), device_id_type=MESH,
        )

    OWNED = {0: (0, 4), 1: (1,), 2: (2,), 3: (3, 5)}
    pl.when(early)(series)
    for role, owner in enumerate(OWNERS):
        @pl.when(m == owner)
        def _(role=role, owner=owner):
            if role == 0:
                halos[0].wait_recv()
            if role == 3:
                halos[2].wait_recv()
            lax.fori_loop(0, 3, lambda i, carry: moments(3 * role + i, i), None)
            for stage, piece in enumerate(OWNED[role]):
                _, base, slot, count, strip_only = PIECES[piece]
                recv = own_recv if strip_only and count == 1 else rs_recv
                iterations(base, slot, count, [(k, recv) for k in range(8) if k != owner or not strip_only])
                for j in range(1, 4):
                    t_copy(piece, (owner + j) % 4, 8 * stage + j).start()
                if stage == 0:
                    pl.semaphore_wait(l_sem, 4)
                for j in range(4):
                    t_copy(piece, 4 + j, 8 * stage + 4 + j).start()

    @pl.when(late & ~trails)
    def _():
        pl.semaphore_wait(right_sem, 1)
        for c in halos[:2]:
            c.start()

    @pl.when(late & leads)
    def _():
        pl.semaphore_wait(left_sem, 1)
        for c in halos[2:]:
            c.start()

    def halo_rows(first):
        for p in (first, first + 1):
            inverse = 1.0 / sp[p]
            for b in range(16):
                weights(p, b, st[b, p], inverse)

    def halo_in():
        for i, c in enumerate(halos):
            if i == 0:
                pl.when(m != OWNERS[0])(c.wait_recv)
            elif i == 2:
                pl.when(m != OWNERS[3])(c.wait_recv)
            else:
                c.wait_recv()
                halo_rows((0, 10)[i // 2])

    def t_in(piece):
        owner = OWNERS[PIECES[piece][0]]
        pl.when(m != owner)(t_copy(piece, owner, 0).wait_recv)

    pl.when(early)(halo_in)
    for piece in range(4):
        t_in(piece)

    def inner_across(b, carry):
        for p in range(2, 10):
            uu[b, p] = relaxed(tp[p], uu[b, p], ww[b, p], row(CURVE, b))
        cells = {p: uu[b, p] for p in range(2, 10)}
        across(b, row, cells, INNER, (up_keep, dn_keep, bot, top), state)
        return carry

    lax.fori_loop(0, 16, inner_across, 0, unroll=4)

    def inner_along(i, carry):
        for j in range(8):
            along(8 * i + j, row, octants[0, 16 * m + 8 * i + j], INNER, fl, state, res)
        return carry

    lax.fori_loop(0, 2, inner_along, 0)
    pl.when(late)(halo_in)
    t_in(4)
    t_in(5)

    for c, when in sends:
        if when is None:
            c.wait_send()
        else:
            pl.when(when)(c.wait_send)
    for c in halos:
        c.wait_send()
    for role, owner in enumerate(OWNERS):
        @pl.when(m == owner)
        def _(role=role, owner=owner):
            for stage, piece in enumerate(OWNED[role]):
                for j in range(1, 8):
                    t_copy(piece, owner, 8 * stage + j).wait_send()


def sweeps(uu, ww, tp, fl, up_keep, dn_keep, bot, top, tab, oc, inner, out, temp_out, state, res, octants, sems):
    signs = pltpu.make_async_copy(oc, octants, sems.at[0])
    signs.start()
    first, count = INNER[0], len(INNER)
    copies = [
        pltpu.make_async_copy(tp.at[pl.ds(2, 8)], temp_out, sems.at[1]),
        pltpu.make_async_copy(inner, out.at[:, pl.ds(first, count)], sems.at[2]),
    ]
    for c in copies:
        c.start()

    def row(table, b):
        return tab[table, pl.ds(b, 1), :]

    def outer_across(b, carry):
        go_x = jnp.broadcast_to(row(GO_X, b), (16, 128)) > 0.5
        cells = {p: uu[b, p] for p in range(2, 10)}
        for p, q in ((1, 10), (0, 11)):
            cells[p] = cells[q] = relaxed(
                jnp.where(go_x, tp[p], tp[q]),
                jnp.where(go_x, uu[b, p], uu[b, q]),
                jnp.where(go_x, ww[b, p], ww[b, q]),
                row(CURVE, b),
            )
        across(b, row, cells, OUTER, (up_keep, dn_keep, bot, top), state)
        return carry

    lax.fori_loop(0, 16, outer_across, 0, unroll=2)
    signs.wait()
    mode = lax.axis_index("mode")

    def outer_along(i, carry):
        for j in range(8):
            along(8 * i + j, row, octants[0, 16 * mode + 8 * i + j], OUTER, fl, state, res)
        for e in range(2):
            pltpu.make_async_copy(
                res.at[pl.ds(8 * i, 8), pl.ds(2 * e, 2)], out.at[pl.ds(8 * i, 8), pl.ds(6 * e, 2)], sems.at[3 + 2 * i + e]
            ).start()
        return carry

    for i in range(2):
        outer_along(i, None)
    for i in range(2):
        for e in range(2):
            copies.append(
                pltpu.make_async_copy(
                    res.at[pl.ds(8 * i, 8), pl.ds(2 * e, 2)], out.at[pl.ds(8 * i, 8), pl.ds(6 * e, 2)], sems.at[3 + 2 * i + e]
                )
            )
    for c in copies:
        c.wait()


def solution(mesh):
    space = mesh.shape["space"]

    def local(energy, void, spacing, walls, octant, warmth, curve, umklapp, isotope, courant):
        flat = lambda v: v.reshape(1, 128)
        vmem = pl.BlockSpec(memory_space=pltpu.VMEM)
        dma = pltpu.SemaphoreType.DMA
        regular = pltpu.SemaphoreType.REGULAR
        held, quarter = (16, 12, 16, 128), (16, 4, 16, 128)
        cells = spacing.shape
        sums = pl.pallas_call(
            functools.partial(kernel, space),
            out_shape=(
                [pltpu.VMEM(held, F32)] * 2
                + [pltpu.VMEM((12, 16, 128), F32)]
                + [pltpu.VMEM(cells, F32)] * 5
                + [pltpu.VMEM((14, 16, 128), F32), pltpu.VMEM((1, 128), jnp.int32), pltpu.VMEM(quarter, F32)]
            ),
            in_specs=[pl.BlockSpec(memory_space=pltpu.HBM)] * 10,
            out_specs=[vmem] * 11,
            scratch_shapes=[
                pltpu.VMEM(quarter, F32),
                pltpu.SMEM((1, 128), jnp.int32),
                pltpu.VMEM(held, F32),
                pltpu.VMEM((12, 16, 128), F32),
                pltpu.VMEM(cells, jnp.int32),
                pltpu.VMEM((2, 8, 128), jnp.int32),
                pltpu.VMEM((32, 128), F32),
                pltpu.VMEM((3, 128), F32),
                pltpu.VMEM(cells, F32),
                pltpu.VMEM((8, 3, 16, 128), F32),
                pltpu.VMEM((TERMS, 3, 16, 128), F32),
                pltpu.VMEM((TERMS, 3, 16, 128), F32),
                pltpu.VMEM((TERMS, 16, 128), F32),
                dma((2,)),
                dma((10,)),
                dma((6,)),
                dma((8,)),
                dma((8,)),
                dma((16,)),
                dma((6,)),
                dma((4,)),
                dma((4,)),
                regular,
                regular,
                regular,
            ],
            compiler_params=pltpu.CompilerParams(
                collective_id=0, has_side_effects=True, vmem_limit_bytes=24 * 1024 * 1024
            ),
        )(
            *[
                pltpu.with_memory_space_constraint(v, pltpu.HBM)
                for v in (
                    energy, void, spacing, walls, flat(octant), flat(warmth), flat(curve), flat(umklapp),
                    flat(isotope), courant,
                )
            ]
        )
        return pl.pallas_call(
            sweeps,
            out_shape=(pltpu.HBM(energy.shape, F32), pltpu.HBM(cells, F32)),
            in_specs=[vmem] * 11,
            out_specs=[pl.BlockSpec(memory_space=pltpu.HBM)] * 2,
            scratch_shapes=[
                pltpu.VMEM(quarter, F32),
                pltpu.VMEM(quarter, F32),
                pltpu.SMEM((1, 128), jnp.int32),
                dma((7,)),
            ],
            compiler_params=pltpu.CompilerParams(vmem_limit_bytes=24 * 1024 * 1024),
        )(*sums)

    in_specs = (
        P("mode", "space", None, None),
        P("space", None, None),
        P("space", None, None),
        P(None, "space", None),
        P(),
        P(),
        P(),
        P(),
        P(),
        P(),
    )
    out_specs = (P("mode", "space", None, None), P("space", None, None))
    return jax.shard_map(local, mesh=mesh, in_specs=in_specs, out_specs=out_specs, check_vma=False)
```

```python
import functools
import math

import jax
import jax.numpy as jnp
from jax import lax
from jax.experimental import pallas as pl
from jax.experimental.pallas import tpu as pltpu
from jax.sharding import PartitionSpec as P

MESH = pl.DeviceIdType.MESH
ITERS = 8
RELAX_WEIGHT = 0.35
HOT_WALL = 1.0
RUN = 8
TERMS = 22
RATE_TERMS = 12
SCALE = 8.0
F32 = jnp.float32

(N_RATE, N_SPEED, WARM_HALF, CURVE, GO_X, GO_Z, X0, X1, X2, CZ, Y0, Y1, Y2, HOT) = range(14)


def sweep_factors(c):
    return 1.0 - 1.5 * c + 0.5 * c * c, 2.0 * c - c * c, 0.5 * c * c - 0.5 * c


OWNERS = (1, 2, 0, 3)
PIECES = ((0, 2, 2, 1, True), (1, 3, 0, 3, True), (2, 6, 0, 3, True), (3, 9, 0, 1, True), (0, 0, 0, 2, False), (3, 10, 1, 2, False))
INNER, OUTER = (2, 3, 4, 5), (0, 1, 6, 7)


def relaxed(t, held, pull, bend):
    x = t * bend
    return held + pull * (jnp.exp2(x) - jnp.exp2(-x))


def across(b, row, cells, rows, walls, state):
    up_keep, dn_keep, bot, top = walls
    depth = lax.broadcasted_iota(jnp.int32, (16, 128), 0)
    go_x = jnp.broadcast_to(row(GO_X, b), (16, 128)) > 0.5
    go_z = jnp.broadcast_to(row(GO_Z, b), (16, 128)) > 0.5
    inflow = jnp.where(go_z, depth, 15 - depth) == 0
    for i, r in enumerate(rows):
        p = r + 2
        near = jnp.where(go_x, cells[p - 1], cells[p + 1])
        far = jnp.where(go_x, cells[p - 2], cells[p + 2])
        a = row(X0, b) * cells[p] + row(X1, b) * near + row(X2, b) * far
        up = jnp.where(go_z, pltpu.roll(a, 1, 0), pltpu.roll(a, 15, 0))
        up = jnp.where(inflow, jnp.where(go_z, bot[r], top[r]) * row(HOT, b), up)
        keep = jnp.where(go_z, up_keep[r], dn_keep[r])
        state[b, i] = a + row(CZ, b) * (up - keep * a)


def along(b, row, octant, rows, fl, state, res):
    shift = jnp.where((octant & 2) == 0, 1, 127)
    twice = jnp.where((octant & 2) == 0, 2, 126)
    for i, r in enumerate(rows):
        a = state[b, i]
        near, far = pltpu.roll(a, shift, 1), pltpu.roll(a, twice, 1)
        res[b, i] = (row(Y0, b) * a + row(Y1, b) * near + row(Y2, b) * far) * fl[r]


def kernel(
    space,
    energy, void, spacing, walls, octant, warmth, curve, umklapp, isotope, courant,
    uu, ww, tp, fl, up_keep, dn_keep, bot, top, tab, oc, res,
    state, octants, st, sp, vd, wl, pv, cr, part, got, mu, mu_slope, zt,
    in_sem, small_sem, rs_send, rs_recv, own_recv, t_send, t_recv, h_send, h_recv, l_sem, left_sem, right_sem,
):
    m, s = lax.axis_index("mode"), lax.axis_index("space")
    left, right = lax.rem(s + space - 1, space), lax.rem(s + 1, space)
    y = lax.rem(m, 4)
    early = m < 4
    late = m >= 4

    def signal(sem, mode, strip):
        pl.semaphore_signal(sem, inc=1, device_id=(mode, strip), device_id_type=MESH)

    barrier = pltpu.get_barrier_semaphore()

    @pl.when(early)
    def _():
        for j in range(4):
            signal(barrier, 4 + j, s)

    @pl.when(m == OWNERS[0])
    def _():
        for k in range(8):
            signal(barrier, 7 - k, left)

    @pl.when(m == OWNERS[3])
    def _():
        for k in range(8):
            signal(barrier, 7 - k, right)

    @pl.when(early)
    def _():
        for j in range(1, 4):
            signal(barrier, lax.rem(m + j, 4), s)
        for strip in (left, right):
            signal(barrier, y, strip)

    small = [
        pltpu.make_async_copy(src, dst, small_sem.at[i])
        for i, (src, dst) in enumerate(
            (
                (spacing, sp.at[pl.ds(2, 8)]),
                (void, vd),
                (umklapp, pv.at[pl.ds(0, 1)]),
                (isotope, pv.at[pl.ds(8, 1)]),
                (courant, cr),
                (warmth, pv.at[pl.ds(16, 1)]),
                (curve, pv.at[pl.ds(24, 1)]),
                (octant, oc),
                (walls, wl),
                (octant, octants),
            )
        )
    ]
    loads = [
        pltpu.make_async_copy(
            energy.at[:, pl.ds(4 * i, 4)], st.at[:, pl.ds(2 + 4 * i, 4)], in_sem.at[i]
        )
        for i in range(2)
    ]
    for c in small[:5]:
        c.start()
    for c in loads:
        c.start()
    for c in small[5:]:
        c.start()

    place = lax.rem(s, RUN)
    leads, trails = place == 0, place == RUN - 1

    @pl.when(late & ~trails)
    def _():
        signal(barrier, m, right)

    @pl.when(late & leads)
    def _():
        signal(barrier, m, left)

    for c in small[:5]:
        c.wait()

    lane = lax.broadcasted_iota(jnp.int32, (16, 128), 1)
    band = lax.broadcasted_iota(jnp.int32, (16, 128), 0) + 16 * m

    def own(vector):
        picked = jnp.where(lane == band, jnp.broadcast_to(vector, (16, 128)), 0.0)
        return jnp.broadcast_to(jnp.sum(picked, axis=1, keepdims=True), (16, 128))

    rate = pv[0:1, :] + pv[8:9, :]
    cx, cy, cz = cr[0:1, :], cr[1:2, :], cr[2:3, :]
    speed = jnp.sqrt(cx * cx + cy * cy + cz * cz)
    tab[N_RATE] = own(-rate)
    tab[N_SPEED] = own(-speed)

    def row(table, b):
        return tab[table, pl.ds(b, 1), :]

    def pass_one(r, carry):
        inverse = 1.0 / sp[2 + r]
        total = jnp.zeros((16, 128), F32)
        for b in range(16):
            kept = jnp.exp(row(N_RATE, b) + row(N_SPEED, b) * inverse)
            total = total + (1.0 - kept) * st[b, 2 + r]
        fluid = (1 - vd[r]).astype(F32)
        fl[r] = fluid
        part[r] = total * fluid
        return carry

    sends = []

    def send(first, count, slot, mode, strip, i, recv, when):
        c = pltpu.make_async_remote_copy(
            part.at[pl.ds(first, count)],
            got.at[m, pl.ds(slot, count)],
            rs_send.at[i],
            recv.at[m],
            device_id=(mode, strip),
            device_id_type=MESH,
        )
        sends.append((c, when))
        if when is None:
            c.start()
        else:
            pl.when(when)(c.start)

    for i in range(2):
        loads[i].wait()
        lax.fori_loop(4 * i, 4 * i + 4, pass_one, 0)

    pl.semaphore_wait(barrier, jnp.where(early, 7, 7 + trails.astype(jnp.int32) - leads.astype(jnp.int32)))
    send(6, 2, 0, OWNERS[0], right, 3, rs_recv, None)
    send(0, 2, 1, OWNERS[3], left, 0, rs_recv, None)
    send(1, 3, 0, OWNERS[1], s, 1, rs_recv, m != OWNERS[1])
    send(4, 3, 0, OWNERS[2], s, 4, rs_recv, m != OWNERS[2])
    send(0, 1, 2, OWNERS[0], s, 2, own_recv, m != OWNERS[0])
    send(7, 1, 0, OWNERS[3], s, 5, own_recv, m != OWNERS[3])

    @pl.when(late)
    def _():
        for k in range(4):
            signal(l_sem, k, s)

    @pl.when(late & ~leads)
    def _():
        signal(right_sem, m, left)

    @pl.when(late & trails)
    def _():
        signal(left_sem, m, right)

    def edges(b, carry):
        for r in OUTER:
            st[b, 2 + r] = st[b, 2 + r] * fl[r]
        return carry

    lax.fori_loop(0, 16, edges, 0)

    halos = []
    for i, (src, dst, strip) in enumerate(((8, 0, right), (2, 10, left))):
        for j, (a, b) in enumerate(
            (
                (sp.at[pl.ds(src, 2)], sp.at[pl.ds(dst, 2)]),
                (st.at[:, pl.ds(src, 2)], st.at[:, pl.ds(dst, 2)]),
            )
        ):
            halos.append(
                pltpu.make_async_remote_copy(
                    a, b, h_send.at[2 * i + j], h_recv.at[2 * i + j], device_id=(m, strip), device_id_type=MESH
                )
            )

    @pl.when(early | trails)
    def _():
        for c in halos[:2]:
            c.start()

    @pl.when(early | ~leads)
    def _():
        for c in halos[2:]:
            c.start()

    for role, slot, first, count in ((0, 2, 0, 1), (1, 0, 1, 3), (2, 0, 4, 3), (3, 0, 7, 1)):
        owner = OWNERS[role]

        @pl.when(m == owner)
        def _(owner=owner, slot=slot, first=first, count=count):
            got[owner, slot : slot + count] = part[first : first + count]

    for c in small[5:]:
        c.wait()

    warm, bend = pv[16:17, :], pv[24:25, :]
    own_warm, own_bend = own(warm), own(bend)
    tab[WARM_HALF] = 0.5 * own_warm / own_bend
    tab[CURVE] = own_bend * (1.0 / math.log(2.0))
    tab[HOT] = (0.5 * own_warm / own_bend) * (jnp.exp(own_bend * HOT_WALL) - jnp.exp(-own_bend * HOT_WALL))
    codes = own(oc[0:1, :].astype(F32)).astype(jnp.int32)
    tab[GO_X] = 1.0 - (codes & 1).astype(F32)
    tab[GO_Z] = 1.0 - (codes // 4).astype(F32)
    tab[X0], tab[X1], tab[X2] = sweep_factors(own(cx))
    tab[Y0], tab[Y1], tab[Y2] = sweep_factors(own(cy))
    tab[CZ] = own(cz)

    def weights(p, b, held, inverse):
        kept = jnp.exp(row(N_RATE, b) + row(N_SPEED, b) * inverse)
        uu[b, p] = kept * held
        ww[b, p] = (1.0 - kept) * row(WARM_HALF, b)

    def pass_two(r, carry):
        inverse = 1.0 / sp[2 + r]
        fluid = fl[r]
        for b in range(16):
            weights(2 + r, b, st[b, 2 + r] * fluid, inverse)
        return carry

    lax.fori_loop(0, 8, pass_two, 0)

    depth = lax.broadcasted_iota(jnp.int32, (16, 128), 0)

    def wall_rows(r, carry):
        low = jnp.broadcast_to(wl[0, pl.ds(r, 1), :], (16, 128))
        high = jnp.broadcast_to(wl[1, pl.ds(r, 1), :], (16, 128))
        up_keep[r] = jnp.where((depth == 15) & (high == 0), 0.0, 1.0)
        dn_keep[r] = jnp.where((depth == 0) & (low == 0), 0.0, 1.0)
        bot[r] = jnp.where((depth == 0) & (low == 2), 1.0, 0.0)
        top[r] = jnp.where((depth == 15) & (high == 2), 1.0, 0.0)
        return carry

    lax.fori_loop(0, 8, wall_rows, 0)

    def series():
        order = lax.broadcasted_iota(jnp.int32, (16, 128), 0)
        rest = jnp.exp(-rate)
        powers = jnp.zeros((16, 128), F32)
        term = -rest
        for j in range(RATE_TERMS):
            value = 1.0 - rest if j == 0 else term
            powers = jnp.where(order == j, jnp.broadcast_to(value, (16, 128)), powers)
            term = term * (-speed) * (1.0 / (j + 1))
        weight = warm
        for k in range(TERMS):
            summed = jnp.sum(powers * weight, axis=1, keepdims=True)
            zt[k] = jnp.broadcast_to(summed, (16, 128))
            weight = weight * (bend * bend) * (SCALE * SCALE / ((2 * k + 2) * (2 * k + 3)))

    def moments(p, i):
        inverse = 1.0 / sp[p]
        for k in range(TERMS):
            value = jnp.broadcast_to(zt[k, RATE_TERMS - 1 : RATE_TERMS, :], (16, 128))
            for j in range(RATE_TERMS - 2, -1, -1):
                value = value * inverse + zt[k, j : j + 1, :]
            mu[k, i] = value
            mu_slope[k, i] = value * (2.0 * k + 1.0)
        return None

    def iterations(base, slot, count, arrivals):
        for k, recv in arrivals:
            pltpu.make_async_remote_copy(
                part.at[pl.ds(0, count)], got.at[k, pl.ds(slot, count)], rs_send.at[0], recv.at[k],
                device_id=(m, s), device_id_type=MESH,
            ).wait_recv()
        rows = slice(slot, slot + count)
        total = got[0, rows]
        for k in range(1, 8):
            total = total + got[k, rows]
        t = RELAX_WEIGHT * total / mu[0, rows]

        def iterate(_, t):
            q = (t * (1.0 / SCALE)) * (t * (1.0 / SCALE))
            square = q * q

            def series_at(table):
                even, odd = table[TERMS - 2, rows], table[TERMS - 1, rows]
                for k in range(TERMS - 4, -1, -2):
                    even = even * square + table[k, rows]
                    odd = odd * square + table[k + 1, rows]
                return even + q * odd

            return t - RELAX_WEIGHT * (t * series_at(mu) - total) / series_at(mu_slope)

        tp[base : base + count] = lax.fori_loop(1, ITERS, iterate, t)

    def t_copy(piece, mode, i):
        _, base, _, count, _ = PIECES[piece]
        return pltpu.make_async_remote_copy(
            tp.at[pl.ds(base, count)], tp.at[pl.ds(base, count)], t_send.at[i], t_recv.at[piece],
            device_id=(mode, s), device_id_type=MESH,
        )

    OWNED = {0: (0, 4), 1: (1,), 2: (2,), 3: (3, 5)}
    pl.when(early)(series)
    for role, owner in enumerate(OWNERS):
        @pl.when(m == owner)
        def _(role=role, owner=owner):
            if role == 0:
                halos[0].wait_recv()
            if role == 3:
                halos[2].wait_recv()
            lax.fori_loop(0, 3, lambda i, carry: moments(3 * role + i, i), None)
            for stage, piece in enumerate(OWNED[role]):
                _, base, slot, count, strip_only = PIECES[piece]
                recv = own_recv if strip_only and count == 1 else rs_recv
                iterations(base, slot, count, [(k, recv) for k in range(8) if k != owner or not strip_only])
                for j in range(1, 4):
                    t_copy(piece, (owner + j) % 4, 8 * stage + j).start()
                if stage == 0:
                    pl.semaphore_wait(l_sem, 4)
                for j in range(4):
                    t_copy(piece, 4 + j, 8 * stage + 4 + j).start()

    @pl.when(late & ~trails)
    def _():
        pl.semaphore_wait(right_sem, 1)
        for c in halos[:2]:
            c.start()

    @pl.when(late & leads)
    def _():
        pl.semaphore_wait(left_sem, 1)
        for c in halos[2:]:
            c.start()

    def halo_rows(first):
        for p in (first, first + 1):
            inverse = 1.0 / sp[p]
            for b in range(16):
                weights(p, b, st[b, p], inverse)

    def halo_in():
        for i, c in enumerate(halos):
            if i == 0:
                pl.when(m != OWNERS[0])(c.wait_recv)
            elif i == 2:
                pl.when(m != OWNERS[3])(c.wait_recv)
            else:
                c.wait_recv()
                halo_rows((0, 10)[i // 2])

    def t_in(piece):
        owner = OWNERS[PIECES[piece][0]]
        pl.when(m != owner)(t_copy(piece, owner, 0).wait_recv)

    pl.when(early)(halo_in)
    for piece in range(4):
        t_in(piece)

    def inner_across(b, carry):
        for p in range(2, 10):
            uu[b, p] = relaxed(tp[p], uu[b, p], ww[b, p], row(CURVE, b))
        cells = {p: uu[b, p] for p in range(2, 10)}
        across(b, row, cells, INNER, (up_keep, dn_keep, bot, top), state)
        return carry

    lax.fori_loop(0, 16, inner_across, 0, unroll=4)

    def inner_along(i, carry):
        for j in range(8):
            along(8 * i + j, row, octants[0, 16 * m + 8 * i + j], INNER, fl, state, res)
        return carry

    lax.fori_loop(0, 2, inner_along, 0)
    pl.when(late)(halo_in)
    t_in(4)
    t_in(5)

    for c, when in sends:
        if when is None:
            c.wait_send()
        else:
            pl.when(when)(c.wait_send)
    for c in halos:
        c.wait_send()
    for role, owner in enumerate(OWNERS):
        @pl.when(m == owner)
        def _(role=role, owner=owner):
            for stage, piece in enumerate(OWNED[role]):
                for j in range(1, 8):
                    t_copy(piece, owner, 8 * stage + j).wait_send()


def sweeps(uu, ww, tp, fl, up_keep, dn_keep, bot, top, tab, oc, inner, out, temp_out, state, res, octants, sems):
    signs = pltpu.make_async_copy(oc, octants, sems.at[0])
    signs.start()
    first, count = INNER[0], len(INNER)
    copies = [
        pltpu.make_async_copy(tp.at[pl.ds(2, 8)], temp_out, sems.at[1]),
        pltpu.make_async_copy(inner, out.at[:, pl.ds(first, count)], sems.at[2]),
    ]
    for c in copies:
        c.start()

    def row(table, b):
        return tab[table, pl.ds(b, 1), :]

    def outer_across(b, carry):
        go_x = jnp.broadcast_to(row(GO_X, b), (16, 128)) > 0.5
        cells = {p: uu[b, p] for p in range(2, 10)}
        for p, q in ((1, 10), (0, 11)):
            cells[p] = cells[q] = relaxed(
                jnp.where(go_x, tp[p], tp[q]),
                jnp.where(go_x, uu[b, p], uu[b, q]),
                jnp.where(go_x, ww[b, p], ww[b, q]),
                row(CURVE, b),
            )
        across(b, row, cells, OUTER, (up_keep, dn_keep, bot, top), state)
        return carry

    lax.fori_loop(0, 16, outer_across, 0, unroll=2)
    signs.wait()
    mode = lax.axis_index("mode")

    def outer_along(i, carry):
        for j in range(4):
            along(4 * i + j, row, octants[0, 16 * mode + 4 * i + j], OUTER, fl, state, res)
        for e in range(2):
            pltpu.make_async_copy(
                res.at[pl.ds(4 * i, 4), pl.ds(2 * e, 2)], out.at[pl.ds(4 * i, 4), pl.ds(6 * e, 2)], sems.at[3 + 2 * i + e]
            ).start()
        return carry

    for i in range(4):
        outer_along(i, None)
    for i in range(4):
        for e in range(2):
            copies.append(
                pltpu.make_async_copy(
                    res.at[pl.ds(4 * i, 4), pl.ds(2 * e, 2)], out.at[pl.ds(4 * i, 4), pl.ds(6 * e, 2)], sems.at[3 + 2 * i + e]
                )
            )
    for c in copies:
        c.wait()


def solution(mesh):
    space = mesh.shape["space"]

    def local(energy, void, spacing, walls, octant, warmth, curve, umklapp, isotope, courant):
        flat = lambda v: v.reshape(1, 128)
        vmem = pl.BlockSpec(memory_space=pltpu.VMEM)
        dma = pltpu.SemaphoreType.DMA
        regular = pltpu.SemaphoreType.REGULAR
        held, quarter = (16, 12, 16, 128), (16, 4, 16, 128)
        cells = spacing.shape
        sums = pl.pallas_call(
            functools.partial(kernel, space),
            out_shape=(
                [pltpu.VMEM(held, F32)] * 2
                + [pltpu.VMEM((12, 16, 128), F32)]
                + [pltpu.VMEM(cells, F32)] * 5
                + [pltpu.VMEM((14, 16, 128), F32), pltpu.VMEM((1, 128), jnp.int32), pltpu.VMEM(quarter, F32)]
            ),
            in_specs=[pl.BlockSpec(memory_space=pltpu.HBM)] * 10,
            out_specs=[vmem] * 11,
            scratch_shapes=[
                pltpu.VMEM(quarter, F32),
                pltpu.SMEM((1, 128), jnp.int32),
                pltpu.VMEM(held, F32),
                pltpu.VMEM((12, 16, 128), F32),
                pltpu.VMEM(cells, jnp.int32),
                pltpu.VMEM((2, 8, 128), jnp.int32),
                pltpu.VMEM((32, 128), F32),
                pltpu.VMEM((3, 128), F32),
                pltpu.VMEM(cells, F32),
                pltpu.VMEM((8, 3, 16, 128), F32),
                pltpu.VMEM((TERMS, 3, 16, 128), F32),
                pltpu.VMEM((TERMS, 3, 16, 128), F32),
                pltpu.VMEM((TERMS, 16, 128), F32),
                dma((2,)),
                dma((10,)),
                dma((6,)),
                dma((8,)),
                dma((8,)),
                dma((16,)),
                dma((6,)),
                dma((4,)),
                dma((4,)),
                regular,
                regular,
                regular,
            ],
            compiler_params=pltpu.CompilerParams(
                collective_id=0, has_side_effects=True, vmem_limit_bytes=24 * 1024 * 1024
            ),
        )(
            *[
                pltpu.with_memory_space_constraint(v, pltpu.HBM)
                for v in (
                    energy, void, spacing, walls, flat(octant), flat(warmth), flat(curve), flat(umklapp),
                    flat(isotope), courant,
                )
            ]
        )
        return pl.pallas_call(
            sweeps,
            out_shape=(pltpu.HBM(energy.shape, F32), pltpu.HBM(cells, F32)),
            in_specs=[vmem] * 11,
            out_specs=[pl.BlockSpec(memory_space=pltpu.HBM)] * 2,
            scratch_shapes=[
                pltpu.VMEM(quarter, F32),
                pltpu.VMEM(quarter, F32),
                pltpu.SMEM((1, 128), jnp.int32),
                dma((11,)),
            ],
            compiler_params=pltpu.CompilerParams(vmem_limit_bytes=24 * 1024 * 1024),
        )(*sums)

    in_specs = (
        P("mode", "space", None, None),
        P("space", None, None),
        P("space", None, None),
        P(None, "space", None),
        P(),
        P(),
        P(),
        P(),
        P(),
        P(),
    )
    out_specs = (P("mode", "space", None, None), P("space", None, None))
    return jax.shard_map(local, mesh=mesh, in_specs=in_specs, out_specs=out_specs, check_vma=False)
```

```python
import functools
import math

import jax
import jax.numpy as jnp
from jax import lax
from jax.experimental import pallas as pl
from jax.experimental.pallas import tpu as pltpu
from jax.sharding import PartitionSpec as P

MESH = pl.DeviceIdType.MESH
ITERS = 8
RELAX_WEIGHT = 0.35
HOT_WALL = 1.0
RUN = 8
TERMS = 22
RATE_TERMS = 12
SCALE = 8.0
F32 = jnp.float32

(N_RATE, N_SPEED, WARM_HALF, CURVE, GO_X, GO_Z, X0, X1, X2, CZ, Y0, Y1, Y2, HOT) = range(14)


def sweep_factors(c):
    return 1.0 - 1.5 * c + 0.5 * c * c, 2.0 * c - c * c, 0.5 * c * c - 0.5 * c


OWNERS = (1, 2, 0, 3)
PIECES = ((0, 2, 2, 1, True), (1, 3, 0, 3, True), (2, 6, 0, 3, True), (3, 9, 0, 1, True), (0, 0, 0, 2, False), (3, 10, 1, 2, False))
INNER, OUTER = (2, 3, 4, 5), (0, 1, 6, 7)


def relaxed(t, held, pull, bend):
    x = t * bend
    return held + pull * (jnp.exp2(x) - jnp.exp2(-x))


def across(b, row, cells, rows, walls, state):
    up_keep, dn_keep, bot, top = walls
    depth = lax.broadcasted_iota(jnp.int32, (16, 128), 0)
    go_x = jnp.broadcast_to(row(GO_X, b), (16, 128)) > 0.5
    go_z = jnp.broadcast_to(row(GO_Z, b), (16, 128)) > 0.5
    inflow = jnp.where(go_z, depth, 15 - depth) == 0
    for i, r in enumerate(rows):
        p = r + 2
        near = jnp.where(go_x, cells[p - 1], cells[p + 1])
        far = jnp.where(go_x, cells[p - 2], cells[p + 2])
        a = row(X0, b) * cells[p] + row(X1, b) * near + row(X2, b) * far
        up = jnp.where(go_z, pltpu.roll(a, 1, 0), pltpu.roll(a, 15, 0))
        up = jnp.where(inflow, jnp.where(go_z, bot[r], top[r]) * row(HOT, b), up)
        keep = jnp.where(go_z, up_keep[r], dn_keep[r])
        state[b, i] = a + row(CZ, b) * (up - keep * a)


def along(b, row, octant, rows, fl, state, res):
    shift = jnp.where((octant & 2) == 0, 1, 127)
    twice = jnp.where((octant & 2) == 0, 2, 126)
    for i, r in enumerate(rows):
        a = state[b, i]
        near, far = pltpu.roll(a, shift, 1), pltpu.roll(a, twice, 1)
        res[b, i] = (row(Y0, b) * a + row(Y1, b) * near + row(Y2, b) * far) * fl[r]


def kernel(
    space,
    energy, void, spacing, walls, octant, warmth, curve, umklapp, isotope, courant,
    uu, ww, tp, fl, up_keep, dn_keep, bot, top, tab, oc, res,
    state, octants, st, sp, vd, wl, pv, cr, part, got, mu, mu_slope, zt,
    in_sem, small_sem, rs_send, rs_recv, own_recv, t_send, t_recv, h_send, h_recv, l_sem, left_sem, right_sem,
):
    m, s = lax.axis_index("mode"), lax.axis_index("space")
    left, right = lax.rem(s + space - 1, space), lax.rem(s + 1, space)
    y = lax.rem(m, 4)
    early = m < 4
    late = m >= 4

    def signal(sem, mode, strip):
        pl.semaphore_signal(sem, inc=1, device_id=(mode, strip), device_id_type=MESH)

    barrier = pltpu.get_barrier_semaphore()

    @pl.when(early)
    def _():
        for j in range(4):
            signal(barrier, 4 + j, s)

    @pl.when(m == OWNERS[0])
    def _():
        for k in range(8):
            signal(barrier, 7 - k, left)

    @pl.when(m == OWNERS[3])
    def _():
        for k in range(8):
            signal(barrier, 7 - k, right)

    @pl.when(early)
    def _():
        for j in range(1, 4):
            signal(barrier, lax.rem(m + j, 4), s)
        for strip in (left, right):
            signal(barrier, y, strip)

    small = [
        pltpu.make_async_copy(src, dst, small_sem.at[i])
        for i, (src, dst) in enumerate(
            (
                (spacing, sp.at[pl.ds(2, 8)]),
                (void, vd),
                (umklapp, pv.at[pl.ds(0, 1)]),
                (isotope, pv.at[pl.ds(8, 1)]),
                (courant, cr),
                (warmth, pv.at[pl.ds(16, 1)]),
                (curve, pv.at[pl.ds(24, 1)]),
                (octant, oc),
                (walls, wl),
                (octant, octants),
            )
        )
    ]
    loads = [
        pltpu.make_async_copy(
            energy.at[:, pl.ds(4 * i, 4)], st.at[:, pl.ds(2 + 4 * i, 4)], in_sem.at[i]
        )
        for i in range(2)
    ]
    for c in small[:5]:
        c.start()
    for c in loads:
        c.start()
    for c in small[5:]:
        c.start()

    place = lax.rem(s, RUN)
    leads, trails = place == 0, place == RUN - 1

    @pl.when(late & ~trails)
    def _():
        signal(barrier, m, right)

    @pl.when(late & leads)
    def _():
        signal(barrier, m, left)

    for c in small[:5]:
        c.wait()

    lane = lax.broadcasted_iota(jnp.int32, (16, 128), 1)
    band = lax.broadcasted_iota(jnp.int32, (16, 128), 0) + 16 * m

    def own(vector):
        picked = jnp.where(lane == band, jnp.broadcast_to(vector, (16, 128)), 0.0)
        return jnp.broadcast_to(jnp.sum(picked, axis=1, keepdims=True), (16, 128))

    rate = pv[0:1, :] + pv[8:9, :]
    cx, cy, cz = cr[0:1, :], cr[1:2, :], cr[2:3, :]
    speed = jnp.sqrt(cx * cx + cy * cy + cz * cz)
    tab[N_RATE] = own(-rate)
    tab[N_SPEED] = own(-speed)

    def row(table, b):
        return tab[table, pl.ds(b, 1), :]

    def pass_one(r, carry):
        inverse = 1.0 / sp[2 + r]
        total = jnp.zeros((16, 128), F32)
        for b in range(16):
            kept = jnp.exp(row(N_RATE, b) + row(N_SPEED, b) * inverse)
            total = total + (1.0 - kept) * st[b, 2 + r]
        fluid = (1 - vd[r]).astype(F32)
        fl[r] = fluid
        part[r] = total * fluid
        return carry

    sends = []

    def send(first, count, slot, mode, strip, i, recv, when):
        c = pltpu.make_async_remote_copy(
            part.at[pl.ds(first, count)],
            got.at[m, pl.ds(slot, count)],
            rs_send.at[i],
            recv.at[m],
            device_id=(mode, strip),
            device_id_type=MESH,
        )
        sends.append((c, when))
        if when is None:
            c.start()
        else:
            pl.when(when)(c.start)

    for i in range(2):
        loads[i].wait()
        lax.fori_loop(4 * i, 4 * i + 4, pass_one, 0)

    pl.semaphore_wait(barrier, jnp.where(early, 7, 7 + trails.astype(jnp.int32) - leads.astype(jnp.int32)))
    send(6, 2, 0, OWNERS[0], right, 3, rs_recv, None)
    send(0, 2, 1, OWNERS[3], left, 0, rs_recv, None)
    send(1, 3, 0, OWNERS[1], s, 1, rs_recv, m != OWNERS[1])
    send(4, 3, 0, OWNERS[2], s, 4, rs_recv, m != OWNERS[2])
    send(0, 1, 2, OWNERS[0], s, 2, own_recv, m != OWNERS[0])
    send(7, 1, 0, OWNERS[3], s, 5, own_recv, m != OWNERS[3])

    @pl.when(late)
    def _():
        for k in range(4):
            signal(l_sem, k, s)

    @pl.when(late & ~leads)
    def _():
        signal(right_sem, m, left)

    @pl.when(late & trails)
    def _():
        signal(left_sem, m, right)

    def edges(b, carry):
        for r in OUTER:
            st[b, 2 + r] = st[b, 2 + r] * fl[r]
        return carry

    lax.fori_loop(0, 16, edges, 0)

    halos = []
    for i, (src, dst, strip) in enumerate(((8, 0, right), (2, 10, left))):
        for j, (a, b) in enumerate(
            (
                (sp.at[pl.ds(src, 2)], sp.at[pl.ds(dst, 2)]),
                (st.at[:, pl.ds(src, 2)], st.at[:, pl.ds(dst, 2)]),
            )
        ):
            halos.append(
                pltpu.make_async_remote_copy(
                    a, b, h_send.at[2 * i + j], h_recv.at[2 * i + j], device_id=(m, strip), device_id_type=MESH
                )
            )

    @pl.when(early | trails)
    def _():
        for c in halos[:2]:
            c.start()

    @pl.when(early | ~leads)
    def _():
        for c in halos[2:]:
            c.start()

    for role, slot, first, count in ((0, 2, 0, 1), (1, 0, 1, 3), (2, 0, 4, 3), (3, 0, 7, 1)):
        owner = OWNERS[role]

        @pl.when(m == owner)
        def _(owner=owner, slot=slot, first=first, count=count):
            got[owner, slot : slot + count] = part[first : first + count]

    for c in small[5:]:
        c.wait()

    warm, bend = pv[16:17, :], pv[24:25, :]
    own_warm, own_bend = own(warm), own(bend)
    tab[WARM_HALF] = 0.5 * own_warm / own_bend
    tab[CURVE] = own_bend * (1.0 / math.log(2.0))
    tab[HOT] = (0.5 * own_warm / own_bend) * (jnp.exp(own_bend * HOT_WALL) - jnp.exp(-own_bend * HOT_WALL))
    codes = own(oc[0:1, :].astype(F32)).astype(jnp.int32)
    tab[GO_X] = 1.0 - (codes & 1).astype(F32)
    tab[GO_Z] = 1.0 - (codes // 4).astype(F32)
    tab[X0], tab[X1], tab[X2] = sweep_factors(own(cx))
    tab[Y0], tab[Y1], tab[Y2] = sweep_factors(own(cy))
    tab[CZ] = own(cz)

    def weights(p, b, held, inverse):
        kept = jnp.exp(row(N_RATE, b) + row(N_SPEED, b) * inverse)
        uu[b, p] = kept * held
        ww[b, p] = (1.0 - kept) * row(WARM_HALF, b)

    def pass_two(r, carry):
        inverse = 1.0 / sp[2 + r]
        fluid = fl[r]
        for b in range(16):
            weights(2 + r, b, st[b, 2 + r] * fluid, inverse)
        return carry

    lax.fori_loop(0, 8, pass_two, 0)

    depth = lax.broadcasted_iota(jnp.int32, (16, 128), 0)

    def wall_rows(r, carry):
        low = jnp.broadcast_to(wl[0, pl.ds(r, 1), :], (16, 128))
        high = jnp.broadcast_to(wl[1, pl.ds(r, 1), :], (16, 128))
        up_keep[r] = jnp.where((depth == 15) & (high == 0), 0.0, 1.0)
        dn_keep[r] = jnp.where((depth == 0) & (low == 0), 0.0, 1.0)
        bot[r] = jnp.where((depth == 0) & (low == 2), 1.0, 0.0)
        top[r] = jnp.where((depth == 15) & (high == 2), 1.0, 0.0)
        return carry

    lax.fori_loop(0, 8, wall_rows, 0)

    def series():
        order = lax.broadcasted_iota(jnp.int32, (16, 128), 0)
        rest = jnp.exp(-rate)
        powers = jnp.zeros((16, 128), F32)
        term = -rest
        for j in range(RATE_TERMS):
            value = 1.0 - rest if j == 0 else term
            powers = jnp.where(order == j, jnp.broadcast_to(value, (16, 128)), powers)
            term = term * (-speed) * (1.0 / (j + 1))
        weight = warm
        for k in range(TERMS):
            summed = jnp.sum(powers * weight, axis=1, keepdims=True)
            zt[k] = jnp.broadcast_to(summed, (16, 128))
            weight = weight * (bend * bend) * (SCALE * SCALE / ((2 * k + 2) * (2 * k + 3)))

    def moments(p, i):
        inverse = 1.0 / sp[p]
        for k in range(TERMS):
            value = jnp.broadcast_to(zt[k, RATE_TERMS - 1 : RATE_TERMS, :], (16, 128))
            for j in range(RATE_TERMS - 2, -1, -1):
                value = value * inverse + zt[k, j : j + 1, :]
            mu[k, i] = value
            mu_slope[k, i] = value * (2.0 * k + 1.0)
        return None

    def iterations(base, slot, count, arrivals):
        for k, recv in arrivals:
            pltpu.make_async_remote_copy(
                part.at[pl.ds(0, count)], got.at[k, pl.ds(slot, count)], rs_send.at[0], recv.at[k],
                device_id=(m, s), device_id_type=MESH,
            ).wait_recv()
        rows = slice(slot, slot + count)
        total = got[0, rows]
        for k in range(1, 8):
            total = total + got[k, rows]
        t = RELAX_WEIGHT * total / mu[0, rows]

        def iterate(_, t):
            q = (t * (1.0 / SCALE)) * (t * (1.0 / SCALE))
            square = q * q

            def series_at(table):
                even, odd = table[TERMS - 2, rows], table[TERMS - 1, rows]
                for k in range(TERMS - 4, -1, -2):
                    even = even * square + table[k, rows]
                    odd = odd * square + table[k + 1, rows]
                return even + q * odd

            return t - RELAX_WEIGHT * (t * series_at(mu) - total) / series_at(mu_slope)

        tp[base : base + count] = lax.fori_loop(1, ITERS, iterate, t)

    def t_copy(piece, mode, i):
        _, base, _, count, _ = PIECES[piece]
        return pltpu.make_async_remote_copy(
            tp.at[pl.ds(base, count)], tp.at[pl.ds(base, count)], t_send.at[i], t_recv.at[piece],
            device_id=(mode, s), device_id_type=MESH,
        )

    OWNED = {0: (0, 4), 1: (1,), 2: (2,), 3: (3, 5)}
    pl.when(early)(series)
    for role, owner in enumerate(OWNERS):
        @pl.when(m == owner)
        def _(role=role, owner=owner):
            if role == 0:
                halos[0].wait_recv()
            if role == 3:
                halos[2].wait_recv()
            lax.fori_loop(0, 3, lambda i, carry: moments(3 * role + i, i), None)
            for stage, piece in enumerate(OWNED[role]):
                _, base, slot, count, strip_only = PIECES[piece]
                recv = own_recv if strip_only and count == 1 else rs_recv
                iterations(base, slot, count, [(k, recv) for k in range(8) if k != owner or not strip_only])
                for j in (2, 1, 3):
                    t_copy(piece, (owner + j) % 4, 8 * stage + j).start()
                if stage == 0:
                    pl.semaphore_wait(l_sem, 4)
                for j in (2, 1, 3, 0):
                    t_copy(piece, 4 + (owner + j) % 4, 8 * stage + 4 + j).start()

    @pl.when(late & ~trails)
    def _():
        pl.semaphore_wait(right_sem, 1)
        for c in halos[:2]:
            c.start()

    @pl.when(late & leads)
    def _():
        pl.semaphore_wait(left_sem, 1)
        for c in halos[2:]:
            c.start()

    def halo_rows(first):
        for p in (first, first + 1):
            inverse = 1.0 / sp[p]
            for b in range(16):
                weights(p, b, st[b, p], inverse)

    def halo_in():
        for i, c in enumerate(halos):
            if i == 0:
                pl.when(m != OWNERS[0])(c.wait_recv)
            elif i == 2:
                pl.when(m != OWNERS[3])(c.wait_recv)
            else:
                c.wait_recv()
                halo_rows((0, 10)[i // 2])

    def t_in(piece):
        owner = OWNERS[PIECES[piece][0]]
        pl.when(m != owner)(t_copy(piece, owner, 0).wait_recv)

    pl.when(early)(halo_in)
    for piece in range(4):
        t_in(piece)

    def inner_across(b, carry):
        for p in range(2, 10):
            uu[b, p] = relaxed(tp[p], uu[b, p], ww[b, p], row(CURVE, b))
        cells = {p: uu[b, p] for p in range(2, 10)}
        across(b, row, cells, INNER, (up_keep, dn_keep, bot, top), state)
        return carry

    lax.fori_loop(0, 16, inner_across, 0, unroll=4)

    def inner_along(i, carry):
        for j in range(8):
            along(8 * i + j, row, octants[0, 16 * m + 8 * i + j], INNER, fl, state, res)
        return carry

    lax.fori_loop(0, 2, inner_along, 0)
    pl.when(late)(halo_in)
    t_in(4)
    t_in(5)

    for c, when in sends:
        if when is None:
            c.wait_send()
        else:
            pl.when(when)(c.wait_send)
    for c in halos:
        c.wait_send()
    for role, owner in enumerate(OWNERS):
        @pl.when(m == owner)
        def _(role=role, owner=owner):
            for stage, piece in enumerate(OWNED[role]):
                for j in range(1, 8):
                    t_copy(piece, owner, 8 * stage + j).wait_send()


def sweeps(uu, ww, tp, fl, up_keep, dn_keep, bot, top, tab, oc, inner, out, temp_out, state, res, octants, sems):
    signs = pltpu.make_async_copy(oc, octants, sems.at[0])
    signs.start()
    first, count = INNER[0], len(INNER)
    copies = [
        pltpu.make_async_copy(tp.at[pl.ds(2, 8)], temp_out, sems.at[1]),
        pltpu.make_async_copy(inner, out.at[:, pl.ds(first, count)], sems.at[2]),
    ]
    for c in copies:
        c.start()

    def row(table, b):
        return tab[table, pl.ds(b, 1), :]

    def outer_across(b, carry):
        go_x = jnp.broadcast_to(row(GO_X, b), (16, 128)) > 0.5
        cells = {p: uu[b, p] for p in range(2, 10)}
        for p, q in ((1, 10), (0, 11)):
            cells[p] = cells[q] = relaxed(
                jnp.where(go_x, tp[p], tp[q]),
                jnp.where(go_x, uu[b, p], uu[b, q]),
                jnp.where(go_x, ww[b, p], ww[b, q]),
                row(CURVE, b),
            )
        across(b, row, cells, OUTER, (up_keep, dn_keep, bot, top), state)
        return carry

    lax.fori_loop(0, 16, outer_across, 0, unroll=2)
    signs.wait()
    mode = lax.axis_index("mode")

    def outer_along(i, carry):
        for j in range(8):
            along(8 * i + j, row, octants[0, 16 * mode + 8 * i + j], OUTER, fl, state, res)
        for e in range(2):
            pltpu.make_async_copy(
                res.at[pl.ds(8 * i, 8), pl.ds(2 * e, 2)], out.at[pl.ds(8 * i, 8), pl.ds(6 * e, 2)], sems.at[3 + 2 * i + e]
            ).start()
        return carry

    for i in range(2):
        outer_along(i, None)
    for i in range(2):
        for e in range(2):
            copies.append(
                pltpu.make_async_copy(
                    res.at[pl.ds(8 * i, 8), pl.ds(2 * e, 2)], out.at[pl.ds(8 * i, 8), pl.ds(6 * e, 2)], sems.at[3 + 2 * i + e]
                )
            )
    for c in copies:
        c.wait()


def solution(mesh):
    space = mesh.shape["space"]

    def local(energy, void, spacing, walls, octant, warmth, curve, umklapp, isotope, courant):
        flat = lambda v: v.reshape(1, 128)
        vmem = pl.BlockSpec(memory_space=pltpu.VMEM)
        dma = pltpu.SemaphoreType.DMA
        regular = pltpu.SemaphoreType.REGULAR
        held, quarter = (16, 12, 16, 128), (16, 4, 16, 128)
        cells = spacing.shape
        sums = pl.pallas_call(
            functools.partial(kernel, space),
            out_shape=(
                [pltpu.VMEM(held, F32)] * 2
                + [pltpu.VMEM((12, 16, 128), F32)]
                + [pltpu.VMEM(cells, F32)] * 5
                + [pltpu.VMEM((14, 16, 128), F32), pltpu.VMEM((1, 128), jnp.int32), pltpu.VMEM(quarter, F32)]
            ),
            in_specs=[pl.BlockSpec(memory_space=pltpu.HBM)] * 10,
            out_specs=[vmem] * 11,
            scratch_shapes=[
                pltpu.VMEM(quarter, F32),
                pltpu.SMEM((1, 128), jnp.int32),
                pltpu.VMEM(held, F32),
                pltpu.VMEM((12, 16, 128), F32),
                pltpu.VMEM(cells, jnp.int32),
                pltpu.VMEM((2, 8, 128), jnp.int32),
                pltpu.VMEM((32, 128), F32),
                pltpu.VMEM((3, 128), F32),
                pltpu.VMEM(cells, F32),
                pltpu.VMEM((8, 3, 16, 128), F32),
                pltpu.VMEM((TERMS, 3, 16, 128), F32),
                pltpu.VMEM((TERMS, 3, 16, 128), F32),
                pltpu.VMEM((TERMS, 16, 128), F32),
                dma((2,)),
                dma((10,)),
                dma((6,)),
                dma((8,)),
                dma((8,)),
                dma((16,)),
                dma((6,)),
                dma((4,)),
                dma((4,)),
                regular,
                regular,
                regular,
            ],
            compiler_params=pltpu.CompilerParams(
                collective_id=0, has_side_effects=True, vmem_limit_bytes=24 * 1024 * 1024
            ),
        )(
            *[
                pltpu.with_memory_space_constraint(v, pltpu.HBM)
                for v in (
                    energy, void, spacing, walls, flat(octant), flat(warmth), flat(curve), flat(umklapp),
                    flat(isotope), courant,
                )
            ]
        )
        return pl.pallas_call(
            sweeps,
            out_shape=(pltpu.HBM(energy.shape, F32), pltpu.HBM(cells, F32)),
            in_specs=[vmem] * 11,
            out_specs=[pl.BlockSpec(memory_space=pltpu.HBM)] * 2,
            scratch_shapes=[
                pltpu.VMEM(quarter, F32),
                pltpu.VMEM(quarter, F32),
                pltpu.SMEM((1, 128), jnp.int32),
                dma((7,)),
            ],
            compiler_params=pltpu.CompilerParams(vmem_limit_bytes=24 * 1024 * 1024),
        )(*sums)

    in_specs = (
        P("mode", "space", None, None),
        P("space", None, None),
        P("space", None, None),
        P(None, "space", None),
        P(),
        P(),
        P(),
        P(),
        P(),
        P(),
    )
    out_specs = (P("mode", "space", None, None), P("space", None, None))
    return jax.shard_map(local, mesh=mesh, in_specs=in_specs, out_specs=out_specs, check_vma=False)
```
